32 devices in a mesh: tok: 4 (over z), head: 8 (over y, x, core).
Axes of the slice: x: 2, y: 2, z: 4, core: 2. Of those that a mesh axis runs over, the one named last changes fastest.
Arguments:
- queries: bfloat16 [2048, 16384], P('tok', 'head'), may hold values from -9 to 9
- keys: bfloat16 [2048, 1024], P('tok'), may hold values from -6 to 6
- values: bfloat16 [2048, 1024], P('tok'), may hold values from -6 to 6
- grad_out: bfloat16 [2048, 16384], P('tok', 'head'), may hold values from -6 to 6
- doc_ids: int32 [2048], P('tok'), may hold values from 0 to 5, never falling along the last dimension, each value on 1 to 1024 neighbouring positions
Outputs:
- attn_out: bfloat16 [2048, 16384], P('tok', 'head')
- grad_queries: bfloat16 [2048, 16384], P('tok', 'head')
- grad_keys: bfloat16 [2048, 1024], P(('tok', 'head'))
- grad_values: bfloat16 [2048, 1024], P(('tok', 'head'))
The draws below stay inside these ranges and needn't reach their ends.
All inputs are finite; a program needn't handle non-finite values.
Results may differ from the reference program's by a relative error of at most 0.04.
Values may be sent and summed in bfloat16 or wider, within the bound.
No kernel may reach another device: no remote copies, remote signals or barrier semaphores. Data moves between devices by JAX's collectives and lax.ppermute only.
A program may use at most 64 MiB of HBM per device.

```python
import math
import jax
import jax.numpy as jnp
import numpy as np
from jax import lax

H = 128
KVH = 8
HD = 128
DOCS = 6
TOKENS = 2048


def draw_queries(key, part):
    drawn = jnp.clip(jax.random.normal(jax.random.fold_in(key, 21), (TOKENS, H * HD), jnp.float32), -6.0, 6.0)
    return drawn.astype(jnp.bfloat16)


def draw_keys(key, part):
    drawn = jnp.clip(jax.random.normal(jax.random.fold_in(key, 22), (TOKENS, KVH * HD), jnp.float32), -6.0, 6.0)
    return drawn.astype(jnp.bfloat16)


def block_levels(rng, extent, split, smallest, high):
    gain, own = 1.0, jax.random.fold_in(rng, 6)
    for dim, shards_of in split:
        steps = jnp.exp(jax.random.uniform(jax.random.fold_in(own, dim), (shards_of,), jnp.float32, smallest / len(split), high / len(split)))
        gain = gain * jnp.repeat(steps, extent[dim] // shards_of).reshape([-1 if axis == dim else 1 for axis in range(len(extent))])
    return gain


def length_profile(amount, total, most, skew):
    loads = [(1 << 20) // math.isqrt(standing ** skew) + 1 for standing in range(2, amount + 1)]
    rest, holding = total - most - (amount - 1), [1] * (amount - 1)
    while rest > 0:
        movable = [i for i in range(amount - 1) if holding[i] < most]
        mass, budget = sum([loads[i] for i in movable]), rest
        for i in movable:
            more = min(most - holding[i], max(1, budget * loads[i] // mass), rest)
            holding[i] = holding[i] + more
            rest = rest - more
    return np.array([most] + holding)


def ragged_sizes(stream_key, number_of, total, limit, slope):
    if number_of == 2:
        one = jax.random.randint(stream_key, (), max(1, total - limit), min(limit, total - 1) + 1)
        return jnp.stack([one, total - one])
    tallies = jnp.asarray(length_profile(number_of, total, limit, slope), jnp.int32)
    pairs = (number_of - 1) // 2
    giver, receiver = tallies[1:1 + 2 * pairs:2], tallies[2:2 + 2 * pairs:2]
    slack = jnp.minimum(giver - 1, limit - receiver)
    moved = jax.random.randint(jax.random.fold_in(stream_key, 1), (pairs,), 0, 1 << 20) % (slack + 1)
    tallies = tallies.at[1:1 + 2 * pairs:2].set(giver - moved).at[2:2 + 2 * pairs:2].set(receiver + moved)
    return tallies[jax.random.permutation(jax.random.fold_in(stream_key, 2), number_of)]


def noise(own_key, dims, scale, most, pieces=(), kind=jnp.bfloat16):
    result = scale * jax.random.normal(own_key, dims, jnp.float32)
    if pieces:
        result = result * block_levels(own_key, dims, pieces, -0.22, 0.18)
    return jnp.clip(result, -most, most).astype(kind)


def setup_inputs(seed: int = 0) -> dict:
    key_of = jax.random.split(jax.random.key(seed), 6)
    return {
        "queries": draw_queries(jax.random.fold_in(key_of[5], 71), 0),
        "keys": draw_keys(jax.random.fold_in(key_of[5], 71), 0),
        "values": noise(key_of[2], (TOKENS, KVH * HD), 1.0, 6.0, ((0, 4),)),
        "grad_out": noise(key_of[3], (TOKENS, H * HD), 1.0, 6.0, ((0, 4), (1, 8))),
        "doc_ids": jnp.searchsorted(jnp.cumsum(ragged_sizes(key_of[4], DOCS, TOKENS, TOKENS // 2, 1)), jnp.arange(TOKENS), side="right").astype(jnp.int32),
    }


def reference(queries, keys, values, grad_out, doc_ids):
    score_scale = HD ** -0.5
    group_size = H // KVH
    positions = jnp.arange(TOKENS, dtype=jnp.int32)
    allowed = (doc_ids[None, :] == doc_ids[:, None]) & (positions[None, :] <= positions[:, None])

    def one_head(head_number):
        kv_head = head_number // group_size
        query_h = lax.dynamic_slice_in_dim(queries, head_number * HD, HD, 1)
        grad_h = lax.dynamic_slice_in_dim(grad_out, head_number * HD, HD, 1)
        key_g = lax.dynamic_slice_in_dim(keys, kv_head * HD, HD, 1)
        value_g = lax.dynamic_slice_in_dim(values, kv_head * HD, HD, 1)
        scores = jnp.dot(query_h, key_g.T, preferred_element_type=jnp.float32) * score_scale
        scores = jnp.where(allowed, scores, -1e30)
        row_max = jnp.max(scores, axis=1)
        log_total = row_max + jnp.log(jnp.sum(jnp.exp(scores - row_max[:, None]), axis=1))
        probs = jnp.where(allowed, jnp.exp(scores - log_total[:, None]), 0.0)
        probs_low = probs.astype(jnp.bfloat16)
        output_f = jnp.dot(probs_low, value_g, preferred_element_type=jnp.float32)
        row_delta = jnp.sum(grad_h.astype(jnp.float32) * output_f, axis=1)
        grad_probs = jnp.dot(grad_h, value_g.T, preferred_element_type=jnp.float32)
        grad_scores = (probs * (grad_probs - row_delta[:, None])).astype(jnp.bfloat16)
        grad_query = jnp.dot(grad_scores, key_g, preferred_element_type=jnp.float32) * score_scale
        grad_key = jnp.dot(grad_scores.T, query_h, preferred_element_type=jnp.float32) * score_scale
        grad_value = jnp.dot(probs_low.T, grad_h, preferred_element_type=jnp.float32)
        return output_f.astype(jnp.bfloat16), grad_query.astype(jnp.bfloat16), grad_key, grad_value

    outputs, grad_qs, grad_ks, grad_vs = lax.map(one_head, jnp.arange(H, dtype=jnp.int32))
    attn_out = outputs.transpose(1, 0, 2).reshape(TOKENS, H * HD)
    grad_queries = grad_qs.transpose(1, 0, 2).reshape(TOKENS, H * HD)
    grad_keys = grad_ks.reshape(KVH, group_size, TOKENS, HD).sum(axis=1)
    grad_values = grad_vs.reshape(KVH, group_size, TOKENS, HD).sum(axis=1)
    grad_keys = grad_keys.transpose(1, 0, 2).reshape(TOKENS, KVH * HD).astype(jnp.bfloat16)
    grad_values = grad_values.transpose(1, 0, 2).reshape(TOKENS, KVH * HD).astype(jnp.bfloat16)
    return attn_out, grad_queries, grad_keys, grad_values
```

```python
import functools
import jax
import jax.numpy as jnp
from jax import lax
from jax.experimental import pallas as pl
from jax.experimental.pallas import tpu as pltpu
from jax.sharding import PartitionSpec as P

KVH = 8
HD = 128
TILE = 256
FAR = -(2.0**20)
SCALE = HD ** (-0.5)
LOG2E = 1.4426950408889634
NN = (((1,), (0,)), ((), ()))
NT = (((1,), (1,)), ((), ()))


def dot(a, b, dims):
    return lax.dot_general(a, b, dims, preferred_element_type=jnp.float32)


def attend_kernel(max_n, own, low_ref, q_ref, g_ref, mark_q_ref, k_ref, v_ref, mark_k_ref,
                  o_ref, dq_ref, dk_ref, dv_ref, ka, kt, vt, s_scr, p_scr, dk_acc, dv_acc):
    head = pl.program_id(0)
    tiles = ka.shape[0]

    @pl.when(head == 0)
    def prepare():
        dk_acc[...] = jnp.zeros_like(dk_acc)
        dv_acc[...] = jnp.zeros_like(dv_acc)
        for i in range(tiles):
            rows = pl.ds(i * TILE, TILE)
            ka[i, :, :HD] = k_ref[rows, :]
            ka[i, :, HD:] = mark_k_ref[rows, :]
            kt[i] = k_ref[rows, :].T
            vt[i, :HD, :] = v_ref[rows, :].T
            vt[i, HD:, :] = jnp.ones((16, TILE), jnp.bfloat16)

    row_iota = lax.broadcasted_iota(jnp.int32, (TILE, TILE), 0)
    col_iota = lax.broadcasted_iota(jnp.int32, (TILE, TILE), 1)
    causal = row_iota <= col_iota

    for qt in range(q_ref.shape[0] // TILE):
        low = low_ref[qt]
        count = own + qt + 1 - low

        def block(n):
            rows = pl.ds(qt * TILE, TILE)
            q = q_ref[rows, :]
            qa = jnp.concatenate([q, mark_q_ref[rows, :]], axis=1)
            top = None
            for j in range(n):
                s = dot(ka[low + j], qa, NT)
                if j == n - 1:
                    s = jnp.where(causal, s, FAR)
                s_scr[j] = s
                part = jnp.max(s, axis=0, keepdims=True)
                top = part if top is None else jnp.maximum(top, part)
            shift = top * (SCALE * LOG2E)
            out = None
            for j in range(n):
                p = jnp.exp2(s_scr[j] * (SCALE * LOG2E) - shift).astype(jnp.bfloat16)
                p_scr[j] = p
                part = dot(vt[low + j], p, NN)
                out = part if out is None else out + part
            inv = 1.0 / out[HD:HD + 1, :]
            out_t = out[:HD, :] * inv
            o_ref[rows, :] = out_t.T.astype(jnp.bfloat16)
            g_t = g_ref[rows, :].astype(jnp.float32).T * inv
            delta = jnp.sum(g_t * out_t, axis=0, keepdims=True)
            g_low = g_t.astype(jnp.bfloat16)
            dq = None
            for j in range(n):
                krows = pl.ds(pl.multiple_of((low + j) * TILE, TILE), TILE)
                p = p_scr[j]
                dp = dot(v_ref[krows, :], g_low, NN)
                ds = p * (dp - delta).astype(jnp.bfloat16)
                part = dot(kt[low + j], ds, NN)
                dq = part if dq is None else dq + part
                dv_acc[low + j] += dot(p, g_low, NT)
                dk_acc[low + j] += dot(ds, q, NN)
            dq_ref[rows, :] = (dq * SCALE).T.astype(jnp.bfloat16)

        for n in range(1, max_n + 1):
            pl.when(count == n)(functools.partial(block, n))

    @pl.when(head == pl.num_programs(0) - 1)
    def finish():
        for i in range(tiles):
            rows = pl.ds(i * TILE, TILE)
            dk_ref[rows, :] = (dk_acc[i] * SCALE).astype(jnp.bfloat16)
            dv_ref[rows, :] = dv_acc[i].astype(jnp.bfloat16)


def attend(queries, grad_out, key_win, value_win, docs_win, prev):
    rows, width = queries.shape
    heads = width // HD
    win = key_win.shape[0]
    tiles = win // TILE
    own = prev * rows // TILE
    max_n = min(own, (prev * rows + TILE - 1) // TILE) + 1
    lanes = jnp.arange(HD, dtype=docs_win.dtype)
    mark_k = jnp.where(docs_win[:, None] == lanes[None, :], 0.0, FAR).astype(jnp.bfloat16)
    mark_q = (docs_win[prev * rows:, None] == lanes[None, :]).astype(jnp.bfloat16)
    firsts = docs_win[prev * rows::TILE]
    low = jnp.sum((docs_win[None, :] < firsts[:, None]).astype(jnp.int32), axis=1) // TILE
    tile_heads = pl.BlockSpec((rows, HD), lambda h, low: (0, h))
    whole = lambda r, c: pl.BlockSpec((r, c), lambda h, low: (0, 0))
    return pl.pallas_call(
        functools.partial(attend_kernel, max_n, own),
        grid_spec=pltpu.PrefetchScalarGridSpec(
            num_scalar_prefetch=1,
            grid=(heads,),
            in_specs=[tile_heads, tile_heads, whole(rows, HD), whole(win, HD), whole(win, HD), whole(win, HD)],
            out_specs=[tile_heads, tile_heads, whole(win, HD), whole(win, HD)],
            scratch_shapes=[
                pltpu.VMEM((tiles, TILE, 2 * HD), jnp.bfloat16),
                pltpu.VMEM((tiles, HD, TILE), jnp.bfloat16),
                pltpu.VMEM((tiles, HD + 16, TILE), jnp.bfloat16),
                pltpu.VMEM((max_n, TILE, TILE), jnp.float32),
                pltpu.VMEM((max_n, TILE, TILE), jnp.bfloat16),
                pltpu.VMEM((tiles, TILE, HD), jnp.float32),
                pltpu.VMEM((tiles, TILE, HD), jnp.float32),
            ],
        ),
        out_shape=[
            jax.ShapeDtypeStruct((rows, width), jnp.bfloat16),
            jax.ShapeDtypeStruct((rows, width), jnp.bfloat16),
            jax.ShapeDtypeStruct((win, HD), jnp.bfloat16),
            jax.ShapeDtypeStruct((win, HD), jnp.bfloat16),
        ],
        compiler_params=pltpu.CompilerParams(vmem_limit_bytes=48 * 2**20),
    )(low, queries, grad_out, mark_q, key_win, value_win, mark_k)


def body(queries, keys, values, grad_out, doc_ids):
    tok_count = lax.axis_size("tok")
    head_count = lax.axis_size("head")
    rows = queries.shape[0]
    copy_count = head_count // KVH
    group = lax.axis_index("head") // copy_count
    prev = min(tok_count - 1, -(-(tok_count * rows // 2 - 1) // rows))
    up = [(i, i + 1) for i in range(tok_count - 1)]
    down = [(i + 1, i) for i in range(tok_count - 1)]
    key_own = lax.dynamic_slice_in_dim(keys, group * HD, HD, 1)
    value_own = lax.dynamic_slice_in_dim(values, group * HD, HD, 1)
    docs_own = (doc_ids + 1).astype(jnp.bfloat16)
    doc_rows = rows // (2 * HD)
    sent = jnp.concatenate(
        [
            jnp.concatenate([key_own, value_own], axis=1),
            jnp.pad(docs_own.reshape(doc_rows, 2 * HD), ((0, 16 - doc_rows), (0, 0))),
        ],
        axis=0,
    )
    pieces = [sent]
    for _ in range(prev):
        pieces.append(lax.ppermute(pieces[-1], "tok", up))
    pieces = pieces[::-1]
    key_win = jnp.concatenate([p[:rows, :HD] for p in pieces], axis=0)
    value_win = jnp.concatenate([p[:rows, HD:] for p in pieces], axis=0)
    docs_win = jnp.concatenate([p[rows:rows + doc_rows].reshape(rows) for p in pieces], axis=0)
    out, grad_q, dk, dv = attend(queries, grad_out, key_win, value_win, docs_win.astype(jnp.int32), prev)
    both = jnp.concatenate([dk, dv], axis=1)
    total = None
    for i in range(prev + 1):
        mine = both[i * rows:(i + 1) * rows]
        if total is None:
            total = mine
        else:
            got = lax.ppermute(total, "tok", down)
            total = (got.astype(jnp.float32) + mine.astype(jnp.float32)).astype(jnp.bfloat16)
    piece = rows // head_count
    mixed = lax.all_to_all(total.reshape(head_count, piece, 2 * HD), "head", 0, 0, tiled=True)
    summed = mixed.reshape(KVH, copy_count, piece, 2 * HD).astype(jnp.float32).sum(axis=1).astype(jnp.bfloat16)
    final = summed.transpose(1, 0, 2)
    return (
        out,
        grad_q,
        final[:, :, :HD].reshape(piece, KVH * HD),
        final[:, :, HD:].reshape(piece, KVH * HD),
    )


def solution(mesh):
    return jax.shard_map(
        body,
        mesh=mesh,
        in_specs=(P("tok", "head"), P("tok", None), P("tok", None), P("tok", "head"), P("tok")),
        out_specs=(P("tok", "head"), P("tok", "head"), P(("tok", "head"), None), P(("tok", "head"), None)),
        check_vma=False,
    )
```

```python
import functools
import jax
import jax.numpy as jnp
from jax import lax
from jax.experimental import pallas as pl
from jax.experimental.pallas import tpu as pltpu
from jax.sharding import PartitionSpec as P

KVH = 8
HD = 128
TILE = 256
GROUP = 4
LAG = 1
FAR = -(2.0**20)
SCALE = HD ** (-0.5)
LOG2E = 1.4426950408889634
NN = (((1,), (0,)), ((), ()))
NT = (((1,), (1,)), ((), ()))


def dot(a, b, dims):
    return lax.dot_general(a, b, dims, preferred_element_type=jnp.float32)


def attend_kernel(max_n, own, low_ref, q_ref, g_ref, mark_q_ref, k_ref, v_ref, mark_k_ref,
                  o_ref, dq_ref, dk_ref, dv_ref, ka, kt, vt, s_scr, p_scr, ds_scr, dk_acc, dv_acc):
    head = pl.program_id(0)
    tiles = ka.shape[0]

    @pl.when((head == 0) & (pl.program_id(1) == 0))
    def prepare():
        dk_acc[...] = jnp.zeros_like(dk_acc)
        dv_acc[...] = jnp.zeros_like(dv_acc)
        for i in range(tiles):
            rows = pl.ds(i * TILE, TILE)
            ka[i, :, :HD] = k_ref[rows, :]
            ka[i, :, HD:] = mark_k_ref[rows, :]
            kt[i] = k_ref[rows, :].T
            vt[i, :HD, :] = v_ref[rows, :].T
            vt[i, HD:, :] = jnp.ones((16, TILE), jnp.bfloat16)

    row_iota = lax.broadcasted_iota(jnp.int32, (TILE, TILE), 0)
    col_iota = lax.broadcasted_iota(jnp.int32, (TILE, TILE), 1)
    causal = row_iota <= col_iota

    if True:
        qt = pl.program_id(1)
        low = low_ref[qt]
        count = own + qt + 1 - low

        def block(n):
            rows = pl.ds(0, TILE)
            cols = [pl.ds(i * HD, HD) for i in range(GROUP)]
            state = [dict() for _ in range(GROUP)]

            def scores(i):
                st = state[i]
                st["q"] = q_ref[rows, cols[i]]
                qa = jnp.concatenate([st["q"], mark_q_ref[rows, :]], axis=1)
                top = None
                for j in range(n):
                    s = dot(ka[low + j], qa, NT)
                    if j == n - 1:
                        s = jnp.where(causal, s, FAR)
                    s_scr[i, j] = s
                    part = jnp.max(s, axis=0, keepdims=True)
                    top = part if top is None else jnp.maximum(top, part)
                st["shift"] = top * (SCALE * LOG2E)

            def weigh(i):
                st = state[i]
                out = None
                for j in range(n):
                    p = jnp.exp2(s_scr[i, j] * (SCALE * LOG2E) - st["shift"]).astype(jnp.bfloat16)
                    p_scr[i, j] = p
                    part = dot(vt[low + j], p, NN)
                    out = part if out is None else out + part
                inv = 1.0 / out[HD:HD + 1, :]
                out_t = out[:HD, :] * inv
                o_ref[rows, cols[i]] = out_t.T.astype(jnp.bfloat16)
                g_t = g_ref[rows, cols[i]].astype(jnp.float32).T * inv
                st["delta"] = jnp.sum(g_t * out_t, axis=0, keepdims=True)
                st["g"] = g_t.astype(jnp.bfloat16)

            def back(i):
                st = state[i]
                dq = None
                for j in range(n):
                    krows = pl.ds(pl.multiple_of((low + j) * TILE, TILE), TILE)
                    p = p_scr[i, j]
                    dp = dot(v_ref[krows, :], st["g"], NN)
                    ds = p * (dp - st["delta"]).astype(jnp.bfloat16)
                    part = dot(kt[low + j], ds, NN)
                    dq = part if dq is None else dq + part
                    ds_scr[i, j] = ds
                dq_ref[rows, cols[i]] = (dq * SCALE).T.astype(jnp.bfloat16)

            def gather():
                q_all = jnp.concatenate([st["q"] for st in state], axis=0)
                g_all = jnp.concatenate([st["g"] for st in state], axis=1)
                for j in range(n):
                    p_all = jnp.concatenate([p_scr[i, j] for i in range(GROUP)], axis=1)
                    ds_all = jnp.concatenate([ds_scr[i, j] for i in range(GROUP)], axis=1)
                    dv_acc[low + j] += dot(p_all, g_all, NT)
                    dk_acc[low + j] += dot(ds_all, q_all, NN)

            for t in range(GROUP + 2 * LAG):
                if t < GROUP:
                    scores(t)
                if 0 <= t - LAG < GROUP:
                    weigh(t - LAG)
                if 0 <= t - 2 * LAG < GROUP:
                    back(t - 2 * LAG)
            gather()

        for n in range(1, max_n + 1):
            pl.when(count == n)(functools.partial(block, n))

    @pl.when((head == pl.num_programs(0) - 1) & (pl.program_id(1) == pl.num_programs(1) - 1))
    def finish():
        for i in range(tiles):
            rows = pl.ds(i * TILE, TILE)
            dk_ref[rows, :] = (dk_acc[i] * SCALE).astype(jnp.bfloat16)
            dv_ref[rows, :] = dv_acc[i].astype(jnp.bfloat16)


def attend(queries, grad_out, key_win, value_win, docs_win, prev):
    rows, width = queries.shape
    heads = width // HD
    win = key_win.shape[0]
    tiles = win // TILE
    own = prev * rows // TILE
    max_n = min(own, (prev * rows + TILE - 1) // TILE) + 1
    lanes = jnp.arange(HD, dtype=docs_win.dtype)
    mark_k = jnp.where(docs_win[:, None] == lanes[None, :], 0.0, FAR).astype(jnp.bfloat16)
    mark_q = (docs_win[prev * rows:, None] == lanes[None, :]).astype(jnp.bfloat16)
    firsts = docs_win[prev * rows::TILE]
    low = jnp.sum((docs_win[None, :] < firsts[:, None]).astype(jnp.int32), axis=1) // TILE
    tile_heads = pl.BlockSpec((TILE, GROUP * HD), lambda h, t, low: (t, h))
    whole = lambda r, c: pl.BlockSpec((r, c), lambda h, t, low: (0, 0))
    return pl.pallas_call(
        functools.partial(attend_kernel, max_n, own),
        grid_spec=pltpu.PrefetchScalarGridSpec(
            num_scalar_prefetch=1,
            grid=(heads // GROUP, rows // TILE),
            in_specs=[tile_heads, tile_heads, pl.BlockSpec((TILE, HD), lambda h, t, low: (t, 0)), whole(win, HD), whole(win, HD), whole(win, HD)],
            out_specs=[tile_heads, tile_heads, whole(win, HD), whole(win, HD)],
            scratch_shapes=[
                pltpu.VMEM((tiles, TILE, 2 * HD), jnp.bfloat16),
                pltpu.VMEM((tiles, HD, TILE), jnp.bfloat16),
                pltpu.VMEM((tiles, HD + 16, TILE), jnp.bfloat16),
                pltpu.VMEM((GROUP, max_n, TILE, TILE), jnp.float32),
                pltpu.VMEM((GROUP, max_n, TILE, TILE), jnp.bfloat16),
                pltpu.VMEM((GROUP, max_n, TILE, TILE), jnp.bfloat16),
                pltpu.VMEM((tiles, TILE, HD), jnp.float32),
                pltpu.VMEM((tiles, TILE, HD), jnp.float32),
            ],
        ),
        out_shape=[
            jax.ShapeDtypeStruct((rows, width), jnp.bfloat16),
            jax.ShapeDtypeStruct((rows, width), jnp.bfloat16),
            jax.ShapeDtypeStruct((win, HD), jnp.bfloat16),
            jax.ShapeDtypeStruct((win, HD), jnp.bfloat16),
        ],
        compiler_params=pltpu.CompilerParams(vmem_limit_bytes=48 * 2**20),
    )(low, queries, grad_out, mark_q, key_win, value_win, mark_k)


def body(queries, keys, values, grad_out, doc_ids):
    tok_count = lax.axis_size("tok")
    head_count = lax.axis_size("head")
    rows = queries.shape[0]
    copy_count = head_count // KVH
    group = lax.axis_index("head") // copy_count
    prev = min(tok_count - 1, -(-(tok_count * rows // 2 - 1) // rows))
    up = [(i, i + 1) for i in range(tok_count - 1)]
    down = [(i + 1, i) for i in range(tok_count - 1)]
    key_own = lax.dynamic_slice_in_dim(keys, group * HD, HD, 1)
    value_own = lax.dynamic_slice_in_dim(values, group * HD, HD, 1)
    docs_own = (doc_ids + 1).astype(jnp.bfloat16)
    doc_rows = rows // (2 * HD)
    sent = jnp.concatenate(
        [
            jnp.concatenate([key_own, value_own], axis=1),
            jnp.pad(docs_own.reshape(doc_rows, 2 * HD), ((0, 16 - doc_rows), (0, 0))),
        ],
        axis=0,
    )
    pieces = [sent]
    for _ in range(prev):
        pieces.append(lax.ppermute(pieces[-1], "tok", up))
    pieces = pieces[::-1]
    key_win = jnp.concatenate([p[:rows, :HD] for p in pieces], axis=0)
    value_win = jnp.concatenate([p[:rows, HD:] for p in pieces], axis=0)
    docs_win = jnp.concatenate([p[rows:rows + doc_rows].reshape(rows) for p in pieces], axis=0)
    out, grad_q, dk, dv = attend(queries, grad_out, key_win, value_win, docs_win.astype(jnp.int32), prev)
    both = jnp.concatenate([dk, dv], axis=1)
    total = None
    for i in range(prev + 1):
        mine = both[i * rows:(i + 1) * rows]
        if total is None:
            total = mine
        else:
            got = lax.ppermute(total, "tok", down)
            total = (got.astype(jnp.float32) + mine.astype(jnp.float32)).astype(jnp.bfloat16)
    piece = rows // head_count
    mixed = lax.all_to_all(total.reshape(head_count, piece, 2 * HD), "head", 0, 0, tiled=True)
    summed = mixed.reshape(KVH, copy_count, piece, 2 * HD).astype(jnp.float32).sum(axis=1).astype(jnp.bfloat16)
    final = summed.transpose(1, 0, 2)
    return (
        out,
        grad_q,
        final[:, :, :HD].reshape(piece, KVH * HD),
        final[:, :, HD:].reshape(piece, KVH * HD),
    )


def solution(mesh):
    return jax.shard_map(
        body,
        mesh=mesh,
        in_specs=(P("tok", "head"), P("tok", None), P("tok", None), P("tok", "head"), P("tok")),
        out_specs=(P("tok", "head"), P("tok", "head"), P(("tok", "head"), None), P(("tok", "head"), None)),
        check_vma=False,
    )
```

```python
import functools
import jax
import jax.numpy as jnp
from jax import lax
from jax.experimental import pallas as pl
from jax.experimental.pallas import tpu as pltpu
from jax.sharding import PartitionSpec as P

KVH = 8
HD = 128
TILE = 256
GROUP = 4
LAG = 4
FAR = -(2.0**20)
SCALE = HD ** (-0.5)
SCALE2 = SCALE * 1.4426950408889634
NN = (((1,), (0,)), ((), ()))
NT = (((1,), (1,)), ((), ()))
HEADS = [pl.ds(i * HD, HD) for i in range(GROUP)]


def dot(a, b, dims):
    return lax.dot_general(a, b, dims, preferred_element_type=jnp.float32)


def in_stages(stages, units, lag):
    for t in range(len(units) + (len(stages) - 1) * lag):
        for at, stage in enumerate(stages):
            if 0 <= t - at * lag < len(units):
                stage(*units[t - at * lag])


def tile_rows(i):
    return pl.ds(i * TILE, TILE)


def marks(chunk_ref, i, same, other):
    rows = chunk_ref.shape[0] - 16
    docs = chunk_ref[rows:rows + 16, :].astype(jnp.float32)[i:i + 1, :]
    lanes = lax.broadcasted_iota(jnp.int32, (HD, TILE), 0).astype(jnp.float32)
    return jnp.where(docs == lanes, same, other).T.astype(jnp.bfloat16)


def chunk_tiles(chunk_ref):
    return (chunk_ref.shape[0] - 16) // TILE


def load_scores(chunk_ref, first, ka, vt):
    for i in range(chunk_tiles(chunk_ref)):
        ka[first + i, :, :HD] = chunk_ref[tile_rows(i), :HD]
        ka[first + i, :, HD:] = marks(chunk_ref, i, 0.0, FAR)
        vt[first + i, :HD, :] = chunk_ref[tile_rows(i), HD:].T
        vt[first + i, HD:, :] = jnp.ones((16, TILE), jnp.bfloat16)


def own_forward(q_ref, own_ref, p_ref, st_ref, ka, vt, mark_q, s_scr):
    tiles = chunk_tiles(own_ref)

    @pl.when(pl.program_id(0) == 0)
    def prepare():
        load_scores(own_ref, 0, ka, vt)
        for i in range(tiles):
            mark_q[i] = marks(own_ref, i, 1.0, 0.0)

    causal = lax.broadcasted_iota(jnp.int32, (TILE, TILE), 0) <= lax.broadcasted_iota(
        jnp.int32, (TILE, TILE), 1
    )
    units = [(i, qt) for qt in range(tiles) for i in range(GROUP)]
    shifts = {}

    def scores(i, qt):
        qa = jnp.concatenate([q_ref[tile_rows(qt), HEADS[i]], mark_q[qt]], axis=1)
        top = None
        for j in range(qt + 1):
            s = dot(ka[j], qa, NT)
            if j == qt:
                s = jnp.where(causal, s, FAR)
            s_scr[i, qt, j] = s
            part = jnp.max(s, axis=0, keepdims=True)
            top = part if top is None else jnp.maximum(top, part)
        shifts[i, qt] = top * SCALE2

    def weigh(i, qt):
        for j in range(qt + 1):
            p = jnp.exp2(s_scr[i, qt, j] * SCALE2 - shifts[i, qt]).astype(jnp.bfloat16)
            p_ref[i, qt * (qt + 1) // 2 + j] = p

    def total(i, qt):
        p = jnp.concatenate([p_ref[i, qt * (qt + 1) // 2 + j] for j in range(qt + 1)], axis=0)
        v_t = jnp.concatenate([vt[j] for j in range(qt + 1)], axis=1)
        out = dot(v_t, p, NN)
        st_ref[i, qt, :HD + 8, :] = out[:HD + 8, :]
        st_ref[i, qt, HD + 8:, :] = jnp.broadcast_to(shifts[i, qt], (8, TILE))

    in_stages([scores, weigh, total], units, LAG)


def earlier_part(prev, max_n, first_ref, q_ref, g_ref, st_ref, own_ref, *refs):
    chunk_refs = refs[:prev]
    o_ref, g3_ref, delta_ref, dq_ref = refs[prev:prev + 4]
    sum_refs = refs[prev + 4:2 * prev + 4]
    ka, kt, vn, vt, mark_q, s_scr, p_scr, ds_scr, dk_acc, dv_acc, low_scr = refs[2 * prev + 4:]
    tiles = chunk_tiles(own_ref)
    own = prev * tiles
    step, qt = pl.program_id(0), pl.program_id(1)

    @pl.when((step == 0) & (qt == 0))
    def prepare():
        dk_acc[...] = jnp.zeros_like(dk_acc)
        dv_acc[...] = jnp.zeros_like(dv_acc)
        earlier = [jnp.float32(0.0) for _ in range(tiles)]
        for c in range(prev):
            load_scores(chunk_refs[c], c * tiles, ka, vt)
            rows = tiles * TILE
            docs = chunk_refs[c][rows:rows + 16, :].astype(jnp.float32)[:tiles, :]
            for i in range(tiles):
                kt[c * tiles + i] = chunk_refs[c][tile_rows(i), :HD].T
                vn[c * tiles + i] = chunk_refs[c][tile_rows(i), HD:]
                less = docs < first_ref[i].astype(jnp.float32)
                earlier[i] += jnp.sum(jnp.where(less, 1.0, 0.0))
        for i in range(tiles):
            mark_q[i] = marks(own_ref, i, 1.0, 0.0)
            low_scr[i] = earlier[i].astype(jnp.int32) // TILE

    low = low_scr[qt]
    count = own - low

    def block(n):
        state = [dict() for _ in range(GROUP)]

        def scores(i):
            st = state[i]
            st["q"] = q_ref[:, HEADS[i]]
            old = st_ref[i, 0, HD + 8:HD + 9, :]
            top = None
            if n:
                qa = jnp.concatenate([st["q"], mark_q[qt]], axis=1)
            for j in range(n):
                s = dot(ka[low + j], qa, NT)
                s_scr[i, j] = s
                part = jnp.max(s, axis=0, keepdims=True)
                top = part if top is None else jnp.maximum(top, part)
            st["shift"] = jnp.maximum(old, top * SCALE2) if n else old
            st["alpha"] = jnp.exp2(old - st["shift"])

        def weigh(i):
            st = state[i]
            for j in range(n):
                p = jnp.exp2(s_scr[i, j] * SCALE2 - st["shift"]).astype(jnp.bfloat16)
                p_scr[i, j] = p

        def total(i):
            st = state[i]
            out = st_ref[i, 0, :HD + 8, :] * st["alpha"]
            if n:
                p = jnp.concatenate([p_scr[i, j] for j in range(n)], axis=0)
                v_t = jnp.concatenate([vt[low + j] for j in range(n)], axis=1)
                out = out + dot(v_t, p, NN)[:HD + 8, :]
            inv = 1.0 / out[HD:HD + 1, :]
            out_t = out[:HD, :] * inv
            o_ref[:, HEADS[i]] = out_t.T.astype(jnp.bfloat16)
            g_t = g_ref[:, HEADS[i]].astype(jnp.float32).T * inv
            st["delta"] = jnp.sum(g_t * out_t, axis=0, keepdims=True)
            st["g"] = g_t.astype(jnp.bfloat16)
            g3_ref[i, 0] = (g_t * st["alpha"]).astype(jnp.bfloat16)
            delta_ref[i, 0] = jnp.broadcast_to(st["delta"] * st["alpha"], (8, TILE))

        def slopes(i):
            st = state[i]
            for j in range(n):
                dp = dot(vn[low + j], st["g"], NN)
                ds_scr[i, j] = p_scr[i, j] * (dp - st["delta"]).astype(jnp.bfloat16)

        def back(i):
            if n:
                ds = jnp.concatenate([ds_scr[i, j] for j in range(n)], axis=0)
                k_t = jnp.concatenate([kt[low + j] for j in range(n)], axis=1)
                dq_ref[i, 0] = dot(k_t, ds, NN)
            else:
                dq_ref[i, 0] = jnp.zeros((HD, TILE), jnp.float32)

        in_stages([scores, weigh, total, slopes, back], [(i,) for i in range(GROUP)], LAG)
        if n:
            q_all = jnp.concatenate([st["q"] for st in state], axis=0)
            g_all = jnp.concatenate([st["g"] for st in state], axis=1)
        for j in range(n):
            p_all = jnp.concatenate([p_scr[i, j] for i in range(GROUP)], axis=1)
            ds_all = jnp.concatenate([ds_scr[i, j] for i in range(GROUP)], axis=1)
            dv_acc[low + j] += dot(p_all, g_all, NT)
            dk_acc[low + j] += dot(ds_all, q_all, NN)

    for n in range(max_n + 1):
        pl.when(count == n)(functools.partial(block, n))

    @pl.when((step == pl.num_programs(0) - 1) & (qt == pl.num_programs(1) - 1))
    def finish():
        for c in range(prev):
            for i in range(tiles):
                sum_refs[c][tile_rows(i), :HD] = (dk_acc[c * tiles + i] * SCALE).astype(jnp.bfloat16)
                sum_refs[c][tile_rows(i), HD:] = dv_acc[c * tiles + i].astype(jnp.bfloat16)


def own_backward(q_ref, own_ref, p_ref, g3_ref, delta_ref, dq_part_ref, dq_ref, sum_ref, kt, ds_scr):
    tiles = chunk_tiles(own_ref)

    @pl.when(pl.program_id(0) == 0)
    def prepare():
        sum_ref[...] = jnp.zeros_like(sum_ref)
        for i in range(tiles):
            kt[i] = own_ref[tile_rows(i), :HD].T

    def slopes(i, qt):
        for j in range(qt + 1):
            at = qt * (qt + 1) // 2 + j
            dp = dot(own_ref[tile_rows(j), HD:], g3_ref[i, qt], NN)
            ds_scr[i, at] = p_ref[i, at] * (dp - delta_ref[i, qt, :1, :]).astype(jnp.bfloat16)

    def back(i, qt):
        ds = jnp.concatenate([ds_scr[i, qt * (qt + 1) // 2 + j] for j in range(qt + 1)], axis=0)
        k_t = jnp.concatenate([kt[j] for j in range(qt + 1)], axis=1)
        dq = dq_part_ref[i, qt] + dot(k_t, ds, NN)
        dq_ref[tile_rows(qt), HEADS[i]] = (dq * SCALE).T.astype(jnp.bfloat16)

    for qt in range(tiles):
        for i in range(GROUP):
            slopes(i, qt)
    for qt in range(tiles):
        for i in range(GROUP):
            back(i, qt)
    for j in range(tiles):
        units = [(i, qt) for qt in range(j, tiles) for i in range(GROUP)]
        at = [(i, qt * (qt + 1) // 2 + j) for i, qt in units]
        q_all = jnp.concatenate([q_ref[tile_rows(qt), HEADS[i]] for i, qt in units], axis=0)
        g_all = jnp.concatenate([g3_ref[i, qt] for i, qt in units], axis=1)
        p_all = jnp.concatenate([p_ref[a] for a in at], axis=1)
        ds_all = jnp.concatenate([ds_scr[a] for a in at], axis=1)
        sum_ref[tile_rows(j), HD:] += dot(p_all, g_all, NT)
        sum_ref[tile_rows(j), :HD] += dot(ds_all, q_all, NN) * SCALE


def call(kernel, grid, in_specs, out_specs, outs, scratch, flops, args, scalars=0):
    return pl.pallas_call(
        kernel,
        grid_spec=pltpu.PrefetchScalarGridSpec(
            num_scalar_prefetch=scalars,
            grid=grid,
            in_specs=in_specs,
            out_specs=out_specs,
            scratch_shapes=scratch,
        ),
        out_shape=outs,
        cost_estimate=pl.CostEstimate(flops=flops, bytes_accessed=16 * 2**20, transcendentals=0),
        compiler_params=pltpu.CompilerParams(vmem_limit_bytes=48 * 2**20),
    )(*args)


def shape(*dims, dtype=jnp.bfloat16):
    return jax.ShapeDtypeStruct(dims, dtype)


def forward_own(queries, sent):
    rows, width = queries.shape
    heads, tiles = width // HD, rows // TILE
    pairs = tiles * (tiles + 1) // 2
    work = heads * pairs * TILE * TILE * HD
    return call(
        own_forward,
        (heads // GROUP,),
        [pl.BlockSpec((rows, GROUP * HD), lambda h: (0, h)), pl.BlockSpec(sent.shape, lambda h: (0, 0))],
        [
            pl.BlockSpec((GROUP, pairs, TILE, TILE), lambda h: (h, 0, 0, 0)),
            pl.BlockSpec((GROUP, tiles, HD + 16, TILE), lambda h: (h, 0, 0, 0)),
        ],
        [
            shape(heads, pairs, TILE, TILE),
            shape(heads, tiles, HD + 16, TILE, dtype=jnp.float32),
        ],
        [
            pltpu.VMEM((tiles, TILE, 2 * HD), jnp.bfloat16),
            pltpu.VMEM((tiles, HD + 16, TILE), jnp.bfloat16),
            pltpu.VMEM((tiles, TILE, HD), jnp.bfloat16),
            pltpu.VMEM((GROUP, tiles, tiles, TILE, TILE), jnp.float32),
        ],
        6 * work,
        (queries, sent),
    )


def earlier(queries, grad_out, first, stats, sent, chunks):
    rows, width = queries.shape
    heads, tiles, prev = width // HD, rows // TILE, len(chunks)
    max_n = prev * tiles
    by_head = pl.BlockSpec((TILE, GROUP * HD), lambda h, t, s: (t, h))
    by_unit = lambda r: pl.BlockSpec((GROUP, 1, r, TILE), lambda h, t, s: (h, t, 0, 0))
    whole = lambda r: pl.BlockSpec((r, 2 * HD), lambda h, t, s: (0, 0))
    results = call(
        functools.partial(earlier_part, prev, max_n),
        (heads // GROUP, tiles),
        [by_head, by_head, by_unit(HD + 16)] + [whole(rows + 16)] * (prev + 1),
        [by_head, by_unit(HD), by_unit(8), by_unit(HD)] + [whole(rows)] * prev,
        [
            shape(rows, width),
            shape(heads, tiles, HD, TILE),
            shape(heads, tiles, 8, TILE, dtype=jnp.float32),
            shape(heads, tiles, HD, TILE, dtype=jnp.float32),
        ]
        + [shape(rows, 2 * HD)] * prev,
        [
            pltpu.VMEM((max_n, TILE, 2 * HD), jnp.bfloat16),
            pltpu.VMEM((max_n, HD, TILE), jnp.bfloat16),
            pltpu.VMEM((max_n, TILE, HD), jnp.bfloat16),
            pltpu.VMEM((max_n, HD + 16, TILE), jnp.bfloat16),
            pltpu.VMEM((tiles, TILE, HD), jnp.bfloat16),
            pltpu.VMEM((GROUP, max_n, TILE, TILE), jnp.float32),
            pltpu.VMEM((GROUP, max_n, TILE, TILE), jnp.bfloat16),
            pltpu.VMEM((GROUP, max_n, TILE, TILE), jnp.bfloat16),
            pltpu.VMEM((max_n, TILE, HD), jnp.float32),
            pltpu.VMEM((max_n, TILE, HD), jnp.float32),
            pltpu.SMEM((tiles,), jnp.int32),
        ],
        12 * heads * rows * max_n * TILE * HD,
        (first, queries, grad_out, stats, sent, *chunks),
        scalars=1,
    )
    return results[:4], results[4:]


def backward_own(queries, sent, p_own, g3, delta, dq_part):
    rows, width = queries.shape
    heads, tiles = width // HD, rows // TILE
    pairs = tiles * (tiles + 1) // 2
    work = heads * pairs * TILE * TILE * HD
    by_head = pl.BlockSpec((rows, GROUP * HD), lambda h: (0, h))
    by_unit = lambda a, r: pl.BlockSpec((GROUP, a, r, TILE), lambda h: (h, 0, 0, 0))
    return call(
        own_backward,
        (heads // GROUP,),
        [
            by_head,
            pl.BlockSpec(sent.shape, lambda h: (0, 0)),
            by_unit(pairs, TILE),
            by_unit(tiles, HD),
            by_unit(tiles, 8),
            by_unit(tiles, HD),
        ],
        [by_head, pl.BlockSpec((rows, 2 * HD), lambda h: (0, 0))],
        [shape(rows, width), shape(rows, 2 * HD, dtype=jnp.float32)],
        [
            pltpu.VMEM((tiles, HD, TILE), jnp.bfloat16),
            pltpu.VMEM((GROUP, pairs, TILE, TILE), jnp.bfloat16),
        ],
        8 * work,
        (queries, sent, p_own, g3, delta, dq_part),
    )


def body(queries, keys, values, grad_out, doc_ids):
    tok_count = lax.axis_size("tok")
    head_count = lax.axis_size("head")
    rows = queries.shape[0]
    tiles = rows // TILE
    copy_count = head_count // KVH
    group = lax.axis_index("head") // copy_count
    longest = tok_count * rows // 2
    prev = min(tok_count - 1, -(-(longest - 1) // rows))
    docs = (doc_ids + 1).astype(jnp.bfloat16).reshape(tiles, TILE)
    sent = jnp.concatenate(
        [
            jnp.concatenate(
                [
                    lax.dynamic_slice_in_dim(keys, group * HD, HD, 1),
                    lax.dynamic_slice_in_dim(values, group * HD, HD, 1),
                ],
                axis=1,
            ),
            jnp.pad(docs, ((0, 16 - tiles), (0, 0))),
        ],
        axis=0,
    )
    first = (doc_ids + 1)[::TILE]
    shift_by = lambda x, k: lax.ppermute(
        x, "tok", [(i, i + k) for i in range(max(0, -k), min(tok_count, tok_count - k))]
    )
    chunks = [shift_by(sent, k) for k in range(prev, 0, -1)]
    p_own, stats = forward_own(queries, sent)
    (out, g3, delta, dq_part), sums = earlier(queries, grad_out, first, stats, sent, chunks)
    got = [shift_by(x, -k) for x, k in zip(sums, range(prev, 0, -1))]
    grad_q, total = backward_own(queries, sent, p_own, g3, delta, dq_part)
    for x in got:
        total = total + x.astype(jnp.float32)
    piece = rows // head_count
    mixed = lax.all_to_all(
        total.astype(jnp.bfloat16).reshape(head_count, piece, 2 * HD), "head", 0, 0, tiled=True
    )
    summed = mixed.reshape(KVH, copy_count, piece, 2 * HD).astype(jnp.float32).sum(axis=1).astype(jnp.bfloat16)
    final = summed.transpose(1, 0, 2)
    return (
        out,
        grad_q,
        final[:, :, :HD].reshape(piece, KVH * HD),
        final[:, :, HD:].reshape(piece, KVH * HD),
    )


def solution(mesh):
    return jax.shard_map(
        body,
        mesh=mesh,
        in_specs=(P("tok", "head"), P("tok", None), P("tok", None), P("tok", "head"), P("tok")),
        out_specs=(P("tok", "head"), P("tok", "head"), P(("tok", "head"), None), P(("tok", "head"), None)),
        check_vma=False,
    )
```

```python
import functools
import jax
import jax.numpy as jnp
from jax import lax
from jax.experimental import pallas as pl
from jax.experimental.pallas import tpu as pltpu
from jax.sharding import PartitionSpec as P

KVH = 8
HD = 128
TILE = 256
GROUP = 4
LAG = 4
FAR = -(2.0**20)
SCALE = HD ** (-0.5)
SCALE2 = SCALE * 1.4426950408889634
NN = (((1,), (0,)), ((), ()))
NT = (((1,), (1,)), ((), ()))
HEADS = [pl.ds(i * HD, HD) for i in range(GROUP)]


def dot(a, b, dims):
    return lax.dot_general(a, b, dims, preferred_element_type=jnp.float32)


def in_stages(stages, units, lag):
    for t in range(len(units) + (len(stages) - 1) * lag):
        for at, stage in enumerate(stages):
            if 0 <= t - at * lag < len(units):
                stage(*units[t - at * lag])


def tile_rows(i):
    return pl.ds(i * TILE, TILE)


def marks(chunk_ref, i, same, other):
    rows = chunk_ref.shape[0] - 16
    docs = chunk_ref[rows:rows + 16, :].astype(jnp.float32)[i:i + 1, :]
    lanes = lax.broadcasted_iota(jnp.int32, (HD, TILE), 0).astype(jnp.float32)
    return jnp.where(docs == lanes, same, other).T.astype(jnp.bfloat16)


def chunk_tiles(chunk_ref):
    return (chunk_ref.shape[0] - 16) // TILE


def load_scores(chunk_ref, first, ka, vt):
    for i in range(chunk_tiles(chunk_ref)):
        ka[first + i, :, :HD] = chunk_ref[tile_rows(i), :HD]
        ka[first + i, :, HD:] = marks(chunk_ref, i, 0.0, FAR)
        vt[first + i, :HD, :] = chunk_ref[tile_rows(i), HD:].T
        vt[first + i, HD:, :] = jnp.ones((16, TILE), jnp.bfloat16)


def own_forward(q_ref, own_ref, *refs):
    p_ref, out_ref, st_ref, ka, vt, mark_q, s_scr = refs[-7:]
    _own_forward(q_ref, own_ref, p_ref, out_ref, st_ref, ka, vt, mark_q, s_scr)


def _own_forward(q_ref, own_ref, p_ref, out_ref, st_ref, ka, vt, mark_q, s_scr):
    tiles = chunk_tiles(own_ref)

    @pl.when(pl.program_id(0) == 0)
    def prepare():
        load_scores(own_ref, 0, ka, vt)
        for i in range(tiles):
            mark_q[i] = marks(own_ref, i, 1.0, 0.0)

    causal = lax.broadcasted_iota(jnp.int32, (TILE, TILE), 0) <= lax.broadcasted_iota(
        jnp.int32, (TILE, TILE), 1
    )
    units = [(i, qt) for qt in range(tiles) for i in range(GROUP)]
    shifts = {}

    def scores(i, qt):
        qa = jnp.concatenate([q_ref[tile_rows(qt), HEADS[i]], mark_q[qt]], axis=1)
        top = None
        for j in range(qt + 1):
            s = dot(ka[j], qa, NT)
            if j == qt:
                s = jnp.where(causal, s, FAR)
            s_scr[i, qt, j] = s
            part = jnp.max(s, axis=0, keepdims=True)
            top = part if top is None else jnp.maximum(top, part)
        shifts[i, qt] = top * SCALE2

    def weigh(i, qt):
        for j in range(qt + 1):
            p = jnp.exp2(s_scr[i, qt, j] * SCALE2 - shifts[i, qt]).astype(jnp.bfloat16)
            p_ref[i, qt * (qt + 1) // 2 + j] = p

    def total(i, qt):
        p = jnp.concatenate([p_ref[i, qt * (qt + 1) // 2 + j] for j in range(qt + 1)], axis=0)
        v_t = jnp.concatenate([vt[j] for j in range(qt + 1)], axis=1)
        out = dot(v_t, p, NN)
        out_ref[i, qt] = out[:HD, :].astype(jnp.bfloat16)
        st_ref[i, qt, :8, :] = out[HD:HD + 8, :]
        st_ref[i, qt, 8:, :] = jnp.broadcast_to(shifts[i, qt], (8, TILE))

    in_stages([scores, weigh, total], units, LAG)


def earlier_part(prev, max_n, first_ref, q_ref, g_ref, part_ref, st_ref, own_ref, *refs):
    chunk_refs = refs[:prev]
    o_ref, g3_ref, delta_ref, dq_ref = refs[prev:prev + 4]
    sum_refs = refs[prev + 4:2 * prev + 4]
    ka, kt, vn, vt, mark_q, s_scr, p_scr, ds_scr, dk_acc, dv_acc, low_scr = refs[2 * prev + 4:]
    tiles = chunk_tiles(own_ref)
    own = prev * tiles
    step, qt = pl.program_id(0), pl.program_id(1)

    @pl.when((step == 0) & (qt == 0))
    def prepare():
        dk_acc[...] = jnp.zeros_like(dk_acc)
        dv_acc[...] = jnp.zeros_like(dv_acc)
        earlier = [jnp.float32(0.0) for _ in range(tiles)]
        for c in range(prev):
            load_scores(chunk_refs[c], c * tiles, ka, vt)
            rows = tiles * TILE
            docs = chunk_refs[c][rows:rows + 16, :].astype(jnp.float32)[:tiles, :]
            for i in range(tiles):
                kt[c * tiles + i] = chunk_refs[c][tile_rows(i), :HD].T
                vn[c * tiles + i] = chunk_refs[c][tile_rows(i), HD:]
                less = docs < first_ref[i].astype(jnp.float32)
                earlier[i] += jnp.sum(jnp.where(less, 1.0, 0.0))
        for i in range(tiles):
            mark_q[i] = marks(own_ref, i, 1.0, 0.0)
            low_scr[i] = earlier[i].astype(jnp.int32) // TILE

    low = low_scr[qt]
    count = own - low

    def block(n):
        state = [dict() for _ in range(GROUP)]

        def scores(i):
            st = state[i]
            st["q"] = q_ref[:, HEADS[i]]
            old = st_ref[i, 0, 8:9, :]
            top = None
            if n:
                qa = jnp.concatenate([st["q"], mark_q[qt]], axis=1)
            for j in range(n):
                s = dot(ka[low + j], qa, NT)
                s_scr[i, j] = s
                part = jnp.max(s, axis=0, keepdims=True)
                top = part if top is None else jnp.maximum(top, part)
            st["shift"] = jnp.maximum(old, top * SCALE2) if n else old
            st["alpha"] = jnp.exp2(old - st["shift"])

        def weigh(i):
            st = state[i]
            for j in range(n):
                p = jnp.exp2(s_scr[i, j] * SCALE2 - st["shift"]).astype(jnp.bfloat16)
                p_scr[i, j] = p

        def total(i):
            st = state[i]
            out = part_ref[i, 0].astype(jnp.float32) * st["alpha"]
            row_sum = st_ref[i, 0, :1, :] * st["alpha"]
            if n:
                p = jnp.concatenate([p_scr[i, j] for j in range(n)], axis=0)
                v_t = jnp.concatenate([vt[low + j] for j in range(n)], axis=1)
                both = dot(v_t, p, NN)
                out = out + both[:HD, :]
                row_sum = row_sum + both[HD:HD + 1, :]
            inv = 1.0 / row_sum
            out_t = out * inv
            o_ref[:, HEADS[i]] = out_t.T.astype(jnp.bfloat16)
            g_t = g_ref[:, HEADS[i]].astype(jnp.float32).T * inv
            st["delta"] = jnp.sum(g_t * out_t, axis=0, keepdims=True)
            st["g"] = g_t.astype(jnp.bfloat16)
            g3_ref[i, 0] = (g_t * st["alpha"]).astype(jnp.bfloat16)
            delta_ref[i, 0] = jnp.broadcast_to(st["delta"] * st["alpha"], (8, TILE))

        def slopes(i):
            st = state[i]
            for j in range(n):
                dp = dot(vn[low + j], st["g"], NN)
                ds_scr[i, j] = p_scr[i, j] * (dp - st["delta"]).astype(jnp.bfloat16)

        def back(i):
            if n:
                ds = jnp.concatenate([ds_scr[i, j] for j in range(n)], axis=0)
                k_t = jnp.concatenate([kt[low + j] for j in range(n)], axis=1)
                dq_ref[i, 0] = dot(k_t, ds, NN).astype(jnp.bfloat16)
            else:
                dq_ref[i, 0] = jnp.zeros((HD, TILE), jnp.bfloat16)

        in_stages([scores, weigh, total, slopes, back], [(i,) for i in range(GROUP)], LAG)
        if n:
            q_all = jnp.concatenate([st["q"] for st in state], axis=0)
            g_all = jnp.concatenate([st["g"] for st in state], axis=1)
        for j in range(n):
            p_all = jnp.concatenate([p_scr[i, j] for i in range(GROUP)], axis=1)
            ds_all = jnp.concatenate([ds_scr[i, j] for i in range(GROUP)], axis=1)
            dv_acc[low + j] += dot(p_all, g_all, NT)
            dk_acc[low + j] += dot(ds_all, q_all, NN)

    for n in range(max_n + 1):
        pl.when(count == n)(functools.partial(block, n))

    @pl.when((step == pl.num_programs(0) - 1) & (qt == pl.num_programs(1) - 1))
    def finish():
        for c in range(prev):
            for i in range(tiles):
                sum_refs[c][tile_rows(i), :HD] = (dk_acc[c * tiles + i] * SCALE).astype(jnp.bfloat16)
                sum_refs[c][tile_rows(i), HD:] = dv_acc[c * tiles + i].astype(jnp.bfloat16)


def own_backward(q_ref, own_ref, p_ref, g3_ref, delta_ref, dq_part_ref, dq_ref, sum_ref, kt, ds_scr):
    tiles = chunk_tiles(own_ref)

    @pl.when(pl.program_id(0) == 0)
    def prepare():
        sum_ref[...] = jnp.zeros_like(sum_ref)
        for i in range(tiles):
            kt[i] = own_ref[tile_rows(i), :HD].T

    def slopes(i, qt):
        for j in range(qt + 1):
            at = qt * (qt + 1) // 2 + j
            dp = dot(own_ref[tile_rows(j), HD:], g3_ref[i, qt], NN)
            ds_scr[i, at] = p_ref[i, at] * (dp - delta_ref[i, qt, :1, :]).astype(jnp.bfloat16)

    def back(i, qt):
        ds = jnp.concatenate([ds_scr[i, qt * (qt + 1) // 2 + j] for j in range(qt + 1)], axis=0)
        k_t = jnp.concatenate([kt[j] for j in range(qt + 1)], axis=1)
        dq = dq_part_ref[i, qt].astype(jnp.float32) + dot(k_t, ds, NN)
        dq_ref[tile_rows(qt), HEADS[i]] = (dq * SCALE).T.astype(jnp.bfloat16)

    for qt in range(tiles):
        for i in range(GROUP):
            slopes(i, qt)
    for qt in range(tiles):
        for i in range(GROUP):
            back(i, qt)
    for j in range(tiles):
        units = [(i, qt) for qt in range(j, tiles) for i in range(GROUP)]
        at = [(i, qt * (qt + 1) // 2 + j) for i, qt in units]
        q_all = jnp.concatenate([q_ref[tile_rows(qt), HEADS[i]] for i, qt in units], axis=0)
        g_all = jnp.concatenate([g3_ref[i, qt] for i, qt in units], axis=1)
        p_all = jnp.concatenate([p_ref[a] for a in at], axis=1)
        ds_all = jnp.concatenate([ds_scr[a] for a in at], axis=1)
        sum_ref[tile_rows(j), HD:] += dot(p_all, g_all, NT)
        sum_ref[tile_rows(j), :HD] += dot(ds_all, q_all, NN) * SCALE


def call(kernel, grid, in_specs, out_specs, outs, scratch, flops, args, scalars=0, aliases={}):
    return pl.pallas_call(
        kernel,
        grid_spec=pltpu.PrefetchScalarGridSpec(
            num_scalar_prefetch=scalars,
            grid=grid,
            in_specs=in_specs,
            out_specs=out_specs,
            scratch_shapes=scratch,
        ),
        out_shape=outs,
        input_output_aliases=aliases,
        cost_estimate=pl.CostEstimate(flops=flops, bytes_accessed=16 * 2**20, transcendentals=0),
        compiler_params=pltpu.CompilerParams(vmem_limit_bytes=48 * 2**20),
    )(*args)


def shape(*dims, dtype=jnp.bfloat16):
    return jax.ShapeDtypeStruct(dims, dtype)


def forward_own(queries, sent, step0, steps, before=None):
    rows, width = queries.shape
    heads, tiles = width // HD, rows // TILE
    pairs = tiles * (tiles + 1) // 2
    work = steps * GROUP * pairs * TILE * TILE * HD
    by_unit = lambda a, r: pl.BlockSpec((GROUP, a, r, TILE), lambda h: (h + step0, 0, 0, 0))
    extra, after = ([], ()) if before is None else before
    return call(
        own_forward,
        (steps,),
        [pl.BlockSpec((rows, GROUP * HD), lambda h: (0, h + step0)), pl.BlockSpec(sent.shape, lambda h: (0, 0))]
        + [pl.BlockSpec(memory_space=pl.ANY)] * (len(extra) + len(after)),
        [by_unit(pairs, TILE), by_unit(tiles, HD), by_unit(tiles, 16)],
        [
            shape(heads, pairs, TILE, TILE),
            shape(heads, tiles, HD, TILE),
            shape(heads, tiles, 16, TILE, dtype=jnp.float32),
        ],
        [
            pltpu.VMEM((tiles, TILE, 2 * HD), jnp.bfloat16),
            pltpu.VMEM((tiles, HD + 16, TILE), jnp.bfloat16),
            pltpu.VMEM((tiles, TILE, HD), jnp.bfloat16),
            pltpu.VMEM((GROUP, tiles, tiles, TILE, TILE), jnp.float32),
        ],
        6 * work,
        (queries, sent, *extra, *after),
        aliases={2 + i: i for i in range(len(extra))},
    )


def earlier(queries, grad_out, first, part, stats, sent, chunks):
    rows, width = queries.shape
    heads, tiles, prev = width // HD, rows // TILE, len(chunks)
    max_n = prev * tiles
    by_head = pl.BlockSpec((TILE, GROUP * HD), lambda h, t, s: (t, h))
    by_unit = lambda r: pl.BlockSpec((GROUP, 1, r, TILE), lambda h, t, s: (h, t, 0, 0))
    whole = lambda r: pl.BlockSpec((r, 2 * HD), lambda h, t, s: (0, 0))
    results = call(
        functools.partial(earlier_part, prev, max_n),
        (heads // GROUP, tiles),
        [by_head, by_head, by_unit(HD), by_unit(16)] + [whole(rows + 16)] * (prev + 1),
        [by_head, by_unit(HD), by_unit(8), by_unit(HD)] + [whole(rows)] * prev,
        [
            shape(rows, width),
            shape(heads, tiles, HD, TILE),
            shape(heads, tiles, 8, TILE, dtype=jnp.float32),
            shape(heads, tiles, HD, TILE),
        ]
        + [shape(rows, 2 * HD)] * prev,
        [
            pltpu.VMEM((max_n, TILE, 2 * HD), jnp.bfloat16),
            pltpu.VMEM((max_n, HD, TILE), jnp.bfloat16),
            pltpu.VMEM((max_n, TILE, HD), jnp.bfloat16),
            pltpu.VMEM((max_n, HD + 16, TILE), jnp.bfloat16),
            pltpu.VMEM((tiles, TILE, HD), jnp.bfloat16),
            pltpu.VMEM((GROUP, max_n, TILE, TILE), jnp.float32),
            pltpu.VMEM((GROUP, max_n, TILE, TILE), jnp.bfloat16),
            pltpu.VMEM((GROUP, max_n, TILE, TILE), jnp.bfloat16),
            pltpu.VMEM((max_n, TILE, HD), jnp.float32),
            pltpu.VMEM((max_n, TILE, HD), jnp.float32),
            pltpu.SMEM((tiles,), jnp.int32),
        ],
        12 * heads * rows * max_n * TILE * HD,
        (first, queries, grad_out, part, stats, sent, *chunks),
        scalars=1,
    )
    return results[:4], results[4:]


def backward_own(queries, sent, p_own, g3, delta, dq_part):
    rows, width = queries.shape
    heads, tiles = width // HD, rows // TILE
    pairs = tiles * (tiles + 1) // 2
    work = heads * pairs * TILE * TILE * HD
    by_head = pl.BlockSpec((rows, GROUP * HD), lambda h: (0, h))
    by_unit = lambda a, r: pl.BlockSpec((GROUP, a, r, TILE), lambda h: (h, 0, 0, 0))
    return call(
        own_backward,
        (heads // GROUP,),
        [
            by_head,
            pl.BlockSpec(sent.shape, lambda h: (0, 0)),
            by_unit(pairs, TILE),
            by_unit(tiles, HD),
            by_unit(tiles, 8),
            by_unit(tiles, HD),
        ],
        [by_head, pl.BlockSpec((rows, 2 * HD), lambda h: (0, 0))],
        [shape(rows, width), shape(rows, 2 * HD, dtype=jnp.float32)],
        [
            pltpu.VMEM((tiles, HD, TILE), jnp.bfloat16),
            pltpu.VMEM((GROUP, pairs, TILE, TILE), jnp.bfloat16),
        ],
        8 * work,
        (queries, sent, p_own, g3, delta, dq_part),
    )


def body(queries, keys, values, grad_out, doc_ids):
    tok_count = lax.axis_size("tok")
    head_count = lax.axis_size("head")
    rows = queries.shape[0]
    tiles = rows // TILE
    copy_count = head_count // KVH
    group = lax.axis_index("head") // copy_count
    longest = tok_count * rows // 2
    prev = min(tok_count - 1, -(-(longest - 1) // rows))
    docs = (doc_ids + 1).astype(jnp.bfloat16).reshape(tiles, TILE)
    sent = jnp.concatenate(
        [
            jnp.concatenate(
                [
                    lax.dynamic_slice_in_dim(keys, group * HD, HD, 1),
                    lax.dynamic_slice_in_dim(values, group * HD, HD, 1),
                ],
                axis=1,
            ),
            jnp.pad(docs, ((0, 16 - tiles), (0, 0))),
        ],
        axis=0,
    )
    first = (doc_ids + 1)[::TILE]
    shift_by = lambda x, k: lax.ppermute(
        x, "tok", [(i, i + k) for i in range(max(0, -k), min(tok_count, tok_count - k))]
    )
    steps = queries.shape[1] // (HD * GROUP)
    head_steps = (steps + 1) // 2
    own_part = forward_own(queries, sent, 0, head_steps)
    chunks = [shift_by(sent, 1)]
    own_part, chunks[0] = lax.optimization_barrier((own_part, chunks[0]))
    for _ in range(prev - 1):
        chunks.append(shift_by(chunks[-1], 1))
    if steps > head_steps:
        own_part = forward_own(queries, sent, head_steps, steps - head_steps, (own_part, chunks[:1]))
    p_own, part, stats = own_part
    chunks = chunks[::-1]
    (out, g3, delta, dq_part), sums = earlier(queries, grad_out, first, part, stats, sent, chunks)
    got = [shift_by(x, -k) for x, k in zip(sums, range(prev, 0, -1))]
    grad_q, total = backward_own(queries, sent, p_own, g3, delta, dq_part)
    for x in got:
        total = total + x.astype(jnp.float32)
    piece = rows // head_count
    mixed = lax.all_to_all(
        total.astype(jnp.bfloat16).reshape(head_count, piece, 2 * HD), "head", 0, 0, tiled=True
    )
    summed = mixed.reshape(KVH, copy_count, piece, 2 * HD).astype(jnp.float32).sum(axis=1).astype(jnp.bfloat16)
    final = summed.transpose(1, 0, 2)
    return (
        out,
        grad_q,
        final[:, :, :HD].reshape(piece, KVH * HD),
        final[:, :, HD:].reshape(piece, KVH * HD),
    )


def solution(mesh):
    return jax.shard_map(
        body,
        mesh=mesh,
        in_specs=(P("tok", "head"), P("tok", None), P("tok", None), P("tok", "head"), P("tok")),
        out_specs=(P("tok", "head"), P("tok", "head"), P(("tok", "head"), None), P(("tok", "head"), None)),
        check_vma=False,
    )
```

```python
import functools
import jax
import jax.numpy as jnp
from jax import lax
from jax.experimental import pallas as pl
from jax.experimental.pallas import tpu as pltpu
from jax.sharding import PartitionSpec as P

KVH = 8
HD = 128
TILE = 256
KEYS = 128
GROUP = 4
LAG = 4
FAR = -(2.0**20)
SCALE = HD ** (-0.5)
SCALE2 = SCALE * 1.4426950408889634
NN = (((1,), (0,)), ((), ()))
NT = (((1,), (1,)), ((), ()))
HEADS = [pl.ds(i * HD, HD) for i in range(GROUP)]


def dot(a, b, dims):
    return lax.dot_general(a, b, dims, preferred_element_type=jnp.float32)


def in_stages(stages, units, lag):
    for t in range(len(units) + (len(stages) - 1) * lag):
        for at, stage in enumerate(stages):
            if 0 <= t - at * lag < len(units):
                stage(*units[t - at * lag])


def tile_rows(i):
    return pl.ds(i * TILE, TILE)


def marks(chunk_ref, i, same, other):
    rows = chunk_ref.shape[0] - 16
    docs = chunk_ref[rows:rows + 16, :].astype(jnp.float32)[i:i + 1, :]
    lanes = lax.broadcasted_iota(jnp.int32, (HD, TILE), 0).astype(jnp.float32)
    return jnp.where(docs == lanes, same, other).T.astype(jnp.bfloat16)


def chunk_tiles(chunk_ref):
    return (chunk_ref.shape[0] - 16) // TILE


def load_scores(chunk_ref, first, ka, vt):
    for i in range(chunk_tiles(chunk_ref)):
        ka[first + i, :, :HD] = chunk_ref[tile_rows(i), :HD]
        ka[first + i, :, HD:] = marks(chunk_ref, i, 0.0, FAR)
        vt[first + i, :HD, :] = chunk_ref[tile_rows(i), HD:].T
        vt[first + i, HD:, :] = jnp.ones((16, TILE), jnp.bfloat16)


def own_forward(q_ref, own_ref, *refs):
    p_ref, out_ref, st_ref, ka, vt, mark_q, s_scr = refs[-7:]
    _own_forward(q_ref, own_ref, p_ref, out_ref, st_ref, ka, vt, mark_q, s_scr)


def _own_forward(q_ref, own_ref, p_ref, out_ref, st_ref, ka, vt, mark_q, s_scr):
    tiles = chunk_tiles(own_ref)

    @pl.when(pl.program_id(0) == 0)
    def prepare():
        load_scores(own_ref, 0, ka, vt)
        for i in range(tiles):
            mark_q[i] = marks(own_ref, i, 1.0, 0.0)

    causal = lax.broadcasted_iota(jnp.int32, (TILE, TILE), 0) <= lax.broadcasted_iota(
        jnp.int32, (TILE, TILE), 1
    )
    units = [(i, qt) for qt in range(tiles) for i in range(GROUP)]
    shifts = {}

    def scores(i, qt):
        qa = jnp.concatenate([q_ref[tile_rows(qt), HEADS[i]], mark_q[qt]], axis=1)
        top = None
        for j in range(qt + 1):
            s = dot(ka[j], qa, NT)
            if j == qt:
                s = jnp.where(causal, s, FAR)
            s_scr[i, qt, j] = s
            part = jnp.max(s, axis=0, keepdims=True)
            top = part if top is None else jnp.maximum(top, part)
        shifts[i, qt] = top * SCALE2

    def weigh(i, qt):
        for j in range(qt + 1):
            p = jnp.exp2(s_scr[i, qt, j] * SCALE2 - shifts[i, qt]).astype(jnp.bfloat16)
            p_ref[i, qt * (qt + 1) // 2 + j] = p

    def total(i, qt):
        p = jnp.concatenate([p_ref[i, qt * (qt + 1) // 2 + j] for j in range(qt + 1)], axis=0)
        v_t = jnp.concatenate([vt[j] for j in range(qt + 1)], axis=1)
        out = dot(v_t, p, NN)
        out_ref[i, qt] = out[:HD, :].astype(jnp.bfloat16)
        st_ref[i, qt, :8, :] = out[HD:HD + 8, :]
        st_ref[i, qt, 8:, :] = jnp.broadcast_to(shifts[i, qt], (8, TILE))

    in_stages([scores, weigh, total], units, LAG)


def earlier_part(prev, max_n, first_ref, q_ref, g_ref, part_ref, st_ref, own_ref, *refs):
    chunk_refs = refs[:prev]
    o_ref, g3_ref, delta_ref, dq_ref = refs[prev:prev + 4]
    sum_refs = refs[prev + 4:2 * prev + 4]
    ka, kt, vn, vt, mark_q, s_scr, p_scr, ds_scr, dk_acc, dv_acc, low_scr = refs[2 * prev + 4:]
    tiles = chunk_tiles(own_ref)
    own = prev * tiles * (TILE // KEYS)
    step, qt = pl.program_id(0), pl.program_id(1)

    @pl.when((step == 0) & (qt == 0))
    def prepare():
        dk_acc[...] = jnp.zeros_like(dk_acc)
        dv_acc[...] = jnp.zeros_like(dv_acc)
        earlier = [jnp.float32(0.0) for _ in range(tiles)]
        for c in range(prev):
            for i in range(tiles):
                far = marks(chunk_refs[c], i, 0.0, FAR)
                for h in range(TILE // KEYS):
                    part = pl.ds(i * TILE + h * KEYS, KEYS)
                    at = (c * tiles + i) * (TILE // KEYS) + h
                    ka[at, :, :HD] = chunk_refs[c][part, :HD]
                    ka[at, :, HD:] = far[h * KEYS:(h + 1) * KEYS, :]
                    vt[at, :HD, :] = chunk_refs[c][part, HD:].T
                    vt[at, HD:, :] = jnp.ones((16, KEYS), jnp.bfloat16)
                    kt[at] = chunk_refs[c][part, :HD].T
                    vn[at] = chunk_refs[c][part, HD:]
            rows = tiles * TILE
            docs = chunk_refs[c][rows:rows + 16, :].astype(jnp.float32)[:tiles, :]
            for i in range(tiles):
                less = docs < first_ref[i].astype(jnp.float32)
                earlier[i] += jnp.sum(jnp.where(less, 1.0, 0.0))
        for i in range(tiles):
            mark_q[i] = marks(own_ref, i, 1.0, 0.0)
            low_scr[i] = earlier[i].astype(jnp.int32) // KEYS

    low = low_scr[qt]
    count = own - low

    def block(n):
        state = [dict() for _ in range(GROUP)]

        def scores(i):
            st = state[i]
            st["q"] = q_ref[:, HEADS[i]]
            old = st_ref[i, 0, 8:9, :]
            top = None
            if n:
                qa = jnp.concatenate([st["q"], mark_q[qt]], axis=1)
            if n:
                s = dot(ka[pl.ds(low, n)].reshape(n * KEYS, 2 * HD), qa, NT)
                s_scr[i, :n] = s.reshape(n, KEYS, TILE)
                top = jnp.max(s, axis=0, keepdims=True)
            st["shift"] = jnp.maximum(old, top * SCALE2) if n else old
            st["alpha"] = jnp.exp2(old - st["shift"])

        def weigh(i):
            st = state[i]
            for j in range(n):
                p = jnp.exp2(s_scr[i, j] * SCALE2 - st["shift"]).astype(jnp.bfloat16)
                p_scr[i, j] = p

        def total(i):
            st = state[i]
            out = part_ref[i, 0].astype(jnp.float32) * st["alpha"]
            row_sum = st_ref[i, 0, :1, :] * st["alpha"]
            if n:
                p = jnp.concatenate([p_scr[i, j] for j in range(n)], axis=0)
                v_t = jnp.concatenate([vt[low + j] for j in range(n)], axis=1)
                both = dot(v_t, p, NN)
                out = out + both[:HD, :]
                row_sum = row_sum + both[HD:HD + 1, :]
            inv = 1.0 / row_sum
            out_t = out * inv
            o_ref[:, HEADS[i]] = out_t.T.astype(jnp.bfloat16)
            g_t = g_ref[:, HEADS[i]].astype(jnp.float32).T * inv
            st["delta"] = jnp.sum(g_t * out_t, axis=0, keepdims=True)
            st["g"] = g_t.astype(jnp.bfloat16)
            g3_ref[i, 0] = (g_t * st["alpha"]).astype(jnp.bfloat16)
            delta_ref[i, 0] = jnp.broadcast_to(st["delta"] * st["alpha"], (8, TILE))

        def slopes(i):
            st = state[i]
            if n:
                dp = dot(vn[pl.ds(low, n)].reshape(n * KEYS, HD), st["g"], NN)
                dp = (dp - st["delta"]).astype(jnp.bfloat16).reshape(n, KEYS, TILE)
                ds_scr[i, :n] = p_scr[i, :n] * dp

        def back(i):
            if n:
                ds = jnp.concatenate([ds_scr[i, j] for j in range(n)], axis=0)
                k_t = jnp.concatenate([kt[low + j] for j in range(n)], axis=1)
                dq_ref[i, 0] = dot(k_t, ds, NN).astype(jnp.bfloat16)
            else:
                dq_ref[i, 0] = jnp.zeros((HD, TILE), jnp.bfloat16)

        in_stages([scores, weigh, total, slopes, back], [(i,) for i in range(GROUP)], LAG)
        if n:
            q_all = jnp.concatenate([st["q"] for st in state], axis=0)
            g_all = jnp.concatenate([st["g"] for st in state], axis=1)
        if n:
            at = pl.ds(low, n)
            p_all = jnp.concatenate([p_scr[i, :n].reshape(n * KEYS, TILE) for i in range(GROUP)], axis=1)
            ds_all = jnp.concatenate([ds_scr[i, :n].reshape(n * KEYS, TILE) for i in range(GROUP)], axis=1)
            dv_acc[at] += dot(p_all, g_all, NT).reshape(n, KEYS, HD)
            dk_acc[at] += dot(ds_all, q_all, NN).reshape(n, KEYS, HD)

    for n in range(max_n + 1):
        pl.when(count == n)(functools.partial(block, n))

    @pl.when((step == pl.num_programs(0) - 1) & (qt == pl.num_programs(1) - 1))
    def finish():
        for c in range(prev):
            for i in range(tiles):
                for h in range(TILE // KEYS):
                    part = pl.ds(i * TILE + h * KEYS, KEYS)
                    at = (c * tiles + i) * (TILE // KEYS) + h
                    sum_refs[c][part, :HD] = (dk_acc[at] * SCALE).astype(jnp.bfloat16)
                    sum_refs[c][part, HD:] = dv_acc[at].astype(jnp.bfloat16)


def own_backward(q_ref, own_ref, p_ref, g3_ref, delta_ref, dq_part_ref, dq_ref, sum_ref, kt, ds_scr):
    tiles = chunk_tiles(own_ref)

    @pl.when(pl.program_id(0) == 0)
    def prepare():
        sum_ref[...] = jnp.zeros_like(sum_ref)
        for i in range(tiles):
            kt[i] = own_ref[tile_rows(i), :HD].T

    def slopes(i, qt):
        for j in range(qt + 1):
            at = qt * (qt + 1) // 2 + j
            dp = dot(own_ref[tile_rows(j), HD:], g3_ref[i, qt], NN)
            ds_scr[i, at] = p_ref[i, at] * (dp - delta_ref[i, qt, :1, :]).astype(jnp.bfloat16)

    def back(i, qt):
        ds = jnp.concatenate([ds_scr[i, qt * (qt + 1) // 2 + j] for j in range(qt + 1)], axis=0)
        k_t = jnp.concatenate([kt[j] for j in range(qt + 1)], axis=1)
        dq = dq_part_ref[i, qt].astype(jnp.float32) + dot(k_t, ds, NN)
        dq_ref[tile_rows(qt), HEADS[i]] = (dq * SCALE).T.astype(jnp.bfloat16)

    for qt in range(tiles):
        for i in range(GROUP):
            slopes(i, qt)
    for qt in range(tiles):
        for i in range(GROUP):
            back(i, qt)
    for j in range(tiles):
        units = [(i, qt) for qt in range(j, tiles) for i in range(GROUP)]
        at = [(i, qt * (qt + 1) // 2 + j) for i, qt in units]
        q_all = jnp.concatenate([q_ref[tile_rows(qt), HEADS[i]] for i, qt in units], axis=0)
        g_all = jnp.concatenate([g3_ref[i, qt] for i, qt in units], axis=1)
        p_all = jnp.concatenate([p_ref[a] for a in at], axis=1)
        ds_all = jnp.concatenate([ds_scr[a] for a in at], axis=1)
        sum_ref[tile_rows(j), HD:] += dot(p_all, g_all, NT)
        sum_ref[tile_rows(j), :HD] += dot(ds_all, q_all, NN) * SCALE


def call(kernel, grid, in_specs, out_specs, outs, scratch, flops, args, scalars=0, aliases={}):
    return pl.pallas_call(
        kernel,
        grid_spec=pltpu.PrefetchScalarGridSpec(
            num_scalar_prefetch=scalars,
            grid=grid,
            in_specs=in_specs,
            out_specs=out_specs,
            scratch_shapes=scratch,
        ),
        out_shape=outs,
        input_output_aliases=aliases,
        cost_estimate=pl.CostEstimate(flops=flops, bytes_accessed=16 * 2**20, transcendentals=0),
        compiler_params=pltpu.CompilerParams(vmem_limit_bytes=48 * 2**20),
    )(*args)


def shape(*dims, dtype=jnp.bfloat16):
    return jax.ShapeDtypeStruct(dims, dtype)


def forward_own(queries, sent, step0, steps, before=None):
    rows, width = queries.shape
    heads, tiles = width // HD, rows // TILE
    pairs = tiles * (tiles + 1) // 2
    work = steps * GROUP * pairs * TILE * TILE * HD
    by_unit = lambda a, r: pl.BlockSpec((GROUP, a, r, TILE), lambda h: (h + step0, 0, 0, 0))
    extra, after = ([], ()) if before is None else before
    return call(
        own_forward,
        (steps,),
        [pl.BlockSpec((rows, GROUP * HD), lambda h: (0, h + step0)), pl.BlockSpec(sent.shape, lambda h: (0, 0))]
        + [pl.BlockSpec(memory_space=pl.ANY)] * (len(extra) + len(after)),
        [by_unit(pairs, TILE), by_unit(tiles, HD), by_unit(tiles, 16)],
        [
            shape(heads, pairs, TILE, TILE),
            shape(heads, tiles, HD, TILE),
            shape(heads, tiles, 16, TILE, dtype=jnp.float32),
        ],
        [
            pltpu.VMEM((tiles, TILE, 2 * HD), jnp.bfloat16),
            pltpu.VMEM((tiles, HD + 16, TILE), jnp.bfloat16),
            pltpu.VMEM((tiles, TILE, HD), jnp.bfloat16),
            pltpu.VMEM((GROUP, tiles, tiles, TILE, TILE), jnp.float32),
        ],
        6 * work,
        (queries, sent, *extra, *after),
        aliases={2 + i: i for i in range(len(extra))},
    )


def earlier(queries, grad_out, first, part, stats, sent, chunks):
    rows, width = queries.shape
    heads, tiles, prev = width // HD, rows // TILE, len(chunks)
    max_n = prev * tiles * (TILE // KEYS)
    by_head = pl.BlockSpec((TILE, GROUP * HD), lambda h, t, s: (t, h))
    by_unit = lambda r: pl.BlockSpec((GROUP, 1, r, TILE), lambda h, t, s: (h, t, 0, 0))
    whole = lambda r: pl.BlockSpec((r, 2 * HD), lambda h, t, s: (0, 0))
    results = call(
        functools.partial(earlier_part, prev, max_n),
        (heads // GROUP, tiles),
        [by_head, by_head, by_unit(HD), by_unit(16)] + [whole(rows + 16)] * (prev + 1),
        [by_head, by_unit(HD), by_unit(8), by_unit(HD)] + [whole(rows)] * prev,
        [
            shape(rows, width),
            shape(heads, tiles, HD, TILE),
            shape(heads, tiles, 8, TILE, dtype=jnp.float32),
            shape(heads, tiles, HD, TILE),
        ]
        + [shape(rows, 2 * HD)] * prev,
        [
            pltpu.VMEM((max_n, KEYS, 2 * HD), jnp.bfloat16),
            pltpu.VMEM((max_n, HD, KEYS), jnp.bfloat16),
            pltpu.VMEM((max_n, KEYS, HD), jnp.bfloat16),
            pltpu.VMEM((max_n, HD + 16, KEYS), jnp.bfloat16),
            pltpu.VMEM((tiles, TILE, HD), jnp.bfloat16),
            pltpu.VMEM((GROUP, max_n, KEYS, TILE), jnp.float32),
            pltpu.VMEM((GROUP, max_n, KEYS, TILE), jnp.bfloat16),
            pltpu.VMEM((GROUP, max_n, KEYS, TILE), jnp.bfloat16),
            pltpu.VMEM((max_n, KEYS, HD), jnp.float32),
            pltpu.VMEM((max_n, KEYS, HD), jnp.float32),
            pltpu.SMEM((tiles,), jnp.int32),
        ],
        12 * heads * rows * max_n * KEYS * HD,
        (first, queries, grad_out, part, stats, sent, *chunks),
        scalars=1,
    )
    return results[:4], results[4:]


def backward_own(queries, sent, p_own, g3, delta, dq_part):
    rows, width = queries.shape
    heads, tiles = width // HD, rows // TILE
    pairs = tiles * (tiles + 1) // 2
    work = heads * pairs * TILE * TILE * HD
    by_head = pl.BlockSpec((rows, GROUP * HD), lambda h: (0, h))
    by_unit = lambda a, r: pl.BlockSpec((GROUP, a, r, TILE), lambda h: (h, 0, 0, 0))
    return call(
        own_backward,
        (heads // GROUP,),
        [
            by_head,
            pl.BlockSpec(sent.shape, lambda h: (0, 0)),
            by_unit(pairs, TILE),
            by_unit(tiles, HD),
            by_unit(tiles, 8),
            by_unit(tiles, HD),
        ],
        [by_head, pl.BlockSpec((rows, 2 * HD), lambda h: (0, 0))],
        [shape(rows, width), shape(rows, 2 * HD, dtype=jnp.float32)],
        [
            pltpu.VMEM((tiles, HD, TILE), jnp.bfloat16),
            pltpu.VMEM((GROUP, pairs, TILE, TILE), jnp.bfloat16),
        ],
        8 * work,
        (queries, sent, p_own, g3, delta, dq_part),
    )


def body(queries, keys, values, grad_out, doc_ids):
    tok_count = lax.axis_size("tok")
    head_count = lax.axis_size("head")
    rows = queries.shape[0]
    tiles = rows // TILE
    copy_count = head_count // KVH
    group = lax.axis_index("head") // copy_count
    longest = tok_count * rows // 2
    prev = min(tok_count - 1, -(-(longest - 1) // rows))
    docs = (doc_ids + 1).astype(jnp.bfloat16).reshape(tiles, TILE)
    sent = jnp.concatenate(
        [
            jnp.concatenate(
                [
                    lax.dynamic_slice_in_dim(keys, group * HD, HD, 1),
                    lax.dynamic_slice_in_dim(values, group * HD, HD, 1),
                ],
                axis=1,
            ),
            jnp.pad(docs, ((0, 16 - tiles), (0, 0))),
        ],
        axis=0,
    )
    first = (doc_ids + 1)[::TILE]
    shift_by = lambda x, k: lax.ppermute(
        x, "tok", [(i, i + k) for i in range(max(0, -k), min(tok_count, tok_count - k))]
    )
    steps = queries.shape[1] // (HD * GROUP)
    head_steps = (steps + 1) // 2
    own_part = forward_own(queries, sent, 0, head_steps)
    chunks = [shift_by(sent, 1)]
    own_part, chunks[0] = lax.optimization_barrier((own_part, chunks[0]))
    for _ in range(prev - 1):
        chunks.append(shift_by(chunks[-1], 1))
    if steps > head_steps:
        own_part = forward_own(queries, sent, head_steps, steps - head_steps, (own_part, chunks[:1]))
    p_own, part, stats = own_part
    chunks = chunks[::-1]
    (out, g3, delta, dq_part), sums = earlier(queries, grad_out, first, part, stats, sent, chunks)
    got = [shift_by(x, -k) for x, k in zip(sums, range(prev, 0, -1))]
    grad_q, total = backward_own(queries, sent, p_own, g3, delta, dq_part)
    for x in got:
        total = total + x.astype(jnp.float32)
    piece = rows // head_count
    mixed = lax.all_to_all(
        total.astype(jnp.bfloat16).reshape(head_count, piece, 2 * HD), "head", 0, 0, tiled=True
    )
    summed = mixed.reshape(KVH, copy_count, piece, 2 * HD).astype(jnp.float32).sum(axis=1).astype(jnp.bfloat16)
    final = summed.transpose(1, 0, 2)
    return (
        out,
        grad_q,
        final[:, :, :HD].reshape(piece, KVH * HD),
        final[:, :, HD:].reshape(piece, KVH * HD),
    )


def solution(mesh):
    return jax.shard_map(
        body,
        mesh=mesh,
        in_specs=(P("tok", "head"), P("tok", None), P("tok", None), P("tok", "head"), P("tok")),
        out_specs=(P("tok", "head"), P("tok", "head"), P(("tok", "head"), None), P(("tok", "head"), None)),
        check_vma=False,
    )
```

```python
import functools
import jax
import jax.numpy as jnp
from jax import lax
from jax.experimental import pallas as pl
from jax.experimental.pallas import tpu as pltpu
from jax.sharding import PartitionSpec as P

KVH = 8
HD = 128
TILE = 256
KEYS = 128
GROUP = 4
LAG = 4
FAR = -(2.0**20)
SCALE = HD ** (-0.5)
SCALE2 = SCALE * 1.4426950408889634
NN = (((1,), (0,)), ((), ()))
NT = (((1,), (1,)), ((), ()))
HEADS = [pl.ds(i * HD, HD) for i in range(GROUP)]


def dot(a, b, dims):
    return lax.dot_general(a, b, dims, preferred_element_type=jnp.float32)


def in_stages(stages, units, lag):
    for t in range(len(units) + (len(stages) - 1) * lag):
        for at, stage in enumerate(stages):
            if 0 <= t - at * lag < len(units):
                stage(*units[t - at * lag])


def tile_rows(i):
    return pl.ds(i * TILE, TILE)


def marks(chunk_ref, i, same, other):
    rows = chunk_ref.shape[0] - 16
    docs = chunk_ref[rows:rows + 16, :].astype(jnp.float32)[i:i + 1, :]
    lanes = lax.broadcasted_iota(jnp.int32, (HD, TILE), 0).astype(jnp.float32)
    return jnp.where(docs == lanes, same, other).T.astype(jnp.bfloat16)


def chunk_tiles(chunk_ref):
    return (chunk_ref.shape[0] - 16) // TILE


def load_scores(chunk_ref, first, ka, vt):
    for i in range(chunk_tiles(chunk_ref)):
        ka[first + i, :, :HD] = chunk_ref[tile_rows(i), :HD]
        ka[first + i, :, HD:] = marks(chunk_ref, i, 0.0, FAR)
        vt[first + i, :HD, :] = chunk_ref[tile_rows(i), HD:].T
        vt[first + i, HD:, :] = jnp.ones((16, TILE), jnp.bfloat16)


def own_forward(q_ref, own_ref, *refs):
    p_ref, out_ref, st_ref, ka, vt, mark_q, s_scr = refs[-7:]
    _own_forward(q_ref, own_ref, p_ref, out_ref, st_ref, ka, vt, mark_q, s_scr)


def _own_forward(q_ref, own_ref, p_ref, out_ref, st_ref, ka, vt, mark_q, s_scr):
    tiles = chunk_tiles(own_ref)

    @pl.when(pl.program_id(0) == 0)
    def prepare():
        load_scores(own_ref, 0, ka, vt)
        for i in range(tiles):
            mark_q[i] = marks(own_ref, i, 1.0, 0.0)

    causal = lax.broadcasted_iota(jnp.int32, (TILE, TILE), 0) <= lax.broadcasted_iota(
        jnp.int32, (TILE, TILE), 1
    )
    units = [(i, qt) for qt in range(tiles) for i in range(GROUP)]
    shifts = {}

    def scores(i, qt):
        qa = jnp.concatenate([q_ref[tile_rows(qt), HEADS[i]], mark_q[qt]], axis=1)
        top = None
        for j in range(qt + 1):
            s = dot(ka[j], qa, NT)
            if j == qt:
                s = jnp.where(causal, s, FAR)
            s_scr[i, qt, j] = s
            part = jnp.max(s, axis=0, keepdims=True)
            top = part if top is None else jnp.maximum(top, part)
        shifts[i, qt] = top * SCALE2

    def weigh(i, qt):
        for j in range(qt + 1):
            p = jnp.exp2(s_scr[i, qt, j] * SCALE2 - shifts[i, qt]).astype(jnp.bfloat16)
            p_ref[i, qt * (qt + 1) // 2 + j] = p

    def total(i, qt):
        p = jnp.concatenate([p_ref[i, qt * (qt + 1) // 2 + j] for j in range(qt + 1)], axis=0)
        v_t = jnp.concatenate([vt[j] for j in range(qt + 1)], axis=1)
        out = dot(v_t, p, NN)
        out_ref[i, qt] = out[:HD, :].astype(jnp.bfloat16)
        st_ref[i, qt, :8, :] = out[HD:HD + 8, :]
        st_ref[i, qt, 8:, :] = jnp.broadcast_to(shifts[i, qt], (8, TILE))

    in_stages([scores, weigh, total], units, LAG)


def earlier_part(prev, max_n, first_ref, q_ref, g_ref, part_ref, st_ref, own_ref, *refs):
    chunk_refs = refs[:prev]
    o_ref, g3_ref, delta_ref, dq_ref = refs[prev:prev + 4]
    sum_refs = refs[prev + 4:2 * prev + 4]
    ka, kt, vn, vt, mark_q, s_scr, p_scr, ds_scr, dk_acc, dv_acc, low_scr = refs[2 * prev + 4:]
    tiles = chunk_tiles(own_ref)
    own = prev * tiles * (TILE // KEYS)
    step, qt = pl.program_id(0), pl.program_id(1)

    @pl.when((step == 0) & (qt == 0))
    def prepare():
        dk_acc[...] = jnp.zeros_like(dk_acc)
        dv_acc[...] = jnp.zeros_like(dv_acc)
        earlier = [jnp.float32(0.0) for _ in range(tiles)]
        for c in range(prev):
            for i in range(tiles):
                far = marks(chunk_refs[c], i, 0.0, FAR)
                for h in range(TILE // KEYS):
                    part = pl.ds(i * TILE + h * KEYS, KEYS)
                    at = (c * tiles + i) * (TILE // KEYS) + h
                    ka[at, :, :HD] = chunk_refs[c][part, :HD]
                    ka[at, :, HD:] = far[h * KEYS:(h + 1) * KEYS, :]
                    vt[at, :HD, :] = chunk_refs[c][part, HD:].T
                    vt[at, HD:, :] = jnp.ones((16, KEYS), jnp.bfloat16)
                    kt[at] = chunk_refs[c][part, :HD].T
                    vn[at] = chunk_refs[c][part, HD:]
            rows = tiles * TILE
            docs = chunk_refs[c][rows:rows + 16, :].astype(jnp.float32)[:tiles, :]
            for i in range(tiles):
                less = docs < first_ref[i].astype(jnp.float32)
                earlier[i] += jnp.sum(jnp.where(less, 1.0, 0.0))
        for i in range(tiles):
            mark_q[i] = marks(own_ref, i, 1.0, 0.0)
            low_scr[i] = earlier[i].astype(jnp.int32) // KEYS

    low = low_scr[qt]
    count = own - low

    def block(n):
        state = [dict() for _ in range(GROUP)]

        def scores(i):
            st = state[i]
            st["q"] = q_ref[:, HEADS[i]]
            old = st_ref[i, 0, 8:9, :]
            top = None
            if n:
                qa = jnp.concatenate([st["q"], mark_q[qt]], axis=1)
            if n:
                s = dot(ka[pl.ds(low, n)].reshape(n * KEYS, 2 * HD), qa, NT)
                s_scr[i, :n] = s.reshape(n, KEYS, TILE)
                top = jnp.max(s, axis=0, keepdims=True)
            st["shift"] = jnp.maximum(old, top * SCALE2) if n else old
            st["alpha"] = jnp.exp2(old - st["shift"])

        def weigh(i):
            st = state[i]
            for j in range(n):
                p = jnp.exp2(s_scr[i, j] * SCALE2 - st["shift"]).astype(jnp.bfloat16)
                p_scr[i, j] = p

        def total(i):
            st = state[i]
            out = part_ref[i, 0].astype(jnp.float32) * st["alpha"]
            row_sum = st_ref[i, 0, :1, :] * st["alpha"]
            if n:
                p = jnp.concatenate([p_scr[i, j] for j in range(n)], axis=0)
                v_t = jnp.concatenate([vt[low + j] for j in range(n)], axis=1)
                both = dot(v_t, p, NN)
                out = out + both[:HD, :]
                row_sum = row_sum + both[HD:HD + 1, :]
            inv = 1.0 / row_sum
            out_t = out * inv
            o_ref[:, HEADS[i]] = out_t.T.astype(jnp.bfloat16)
            g_t = g_ref[:, HEADS[i]].astype(jnp.float32).T * inv
            st["delta"] = jnp.sum(g_t * out_t, axis=0, keepdims=True)
            st["g"] = g_t.astype(jnp.bfloat16)
            g3_ref[i, 0] = (g_t * st["alpha"]).astype(jnp.bfloat16)
            delta_ref[i, 0] = jnp.broadcast_to(st["delta"] * st["alpha"], (8, TILE))

        def slopes(i):
            st = state[i]
            if n:
                dp = dot(vn[pl.ds(low, n)].reshape(n * KEYS, HD), st["g"], NN)
                dp = (dp - st["delta"]).astype(jnp.bfloat16).reshape(n, KEYS, TILE)
                ds_scr[i, :n] = p_scr[i, :n] * dp

        def back(i):
            if n:
                ds = jnp.concatenate([ds_scr[i, j] for j in range(n)], axis=0)
                k_t = jnp.concatenate([kt[low + j] for j in range(n)], axis=1)
                dq_ref[i, 0] = dot(k_t, ds, NN).astype(jnp.bfloat16)
            else:
                dq_ref[i, 0] = jnp.zeros((HD, TILE), jnp.bfloat16)

        in_stages([scores, weigh, total, slopes, back], [(i,) for i in range(GROUP)], LAG)
        if n:
            q_all = jnp.concatenate([st["q"] for st in state], axis=0)
            g_all = jnp.concatenate([st["g"] for st in state], axis=1)
        if n:
            at = pl.ds(low, n)
            p_all = jnp.concatenate([p_scr[i, :n].reshape(n * KEYS, TILE) for i in range(GROUP)], axis=1)
            ds_all = jnp.concatenate([ds_scr[i, :n].reshape(n * KEYS, TILE) for i in range(GROUP)], axis=1)
            dv_acc[at] += dot(p_all, g_all, NT).reshape(n, KEYS, HD)
            dk_acc[at] += dot(ds_all, q_all, NN).reshape(n, KEYS, HD)

    for n in range(max_n + 1):
        pl.when(count == n)(functools.partial(block, n))

    @pl.when((step == pl.num_programs(0) - 1) & (qt == pl.num_programs(1) - 1))
    def finish():
        for c in range(prev):
            for i in range(tiles):
                for h in range(TILE // KEYS):
                    part = pl.ds(i * TILE + h * KEYS, KEYS)
                    at = (c * tiles + i) * (TILE // KEYS) + h
                    sum_refs[c][part, :HD] = (dk_acc[at] * SCALE).astype(jnp.bfloat16)
                    sum_refs[c][part, HD:] = dv_acc[at].astype(jnp.bfloat16)


def own_backward(q_ref, own_ref, p_ref, g3_ref, delta_ref, dq_part_ref, dq_ref, sum_ref, kt, ds_scr):
    tiles = chunk_tiles(own_ref)

    @pl.when(pl.program_id(0) == 0)
    def prepare():
        sum_ref[...] = jnp.zeros_like(sum_ref)
        for i in range(tiles):
            kt[i] = own_ref[tile_rows(i), :HD].T

    def slopes(i, qt):
        for j in range(qt + 1):
            at = qt * (qt + 1) // 2 + j
            dp = dot(own_ref[tile_rows(j), HD:], g3_ref[i, qt], NN)
            ds_scr[i, at] = p_ref[i, at] * (dp - delta_ref[i, qt, :1, :]).astype(jnp.bfloat16)

    def back(i, qt):
        ds = jnp.concatenate([ds_scr[i, qt * (qt + 1) // 2 + j] for j in range(qt + 1)], axis=0)
        k_t = jnp.concatenate([kt[j] for j in range(qt + 1)], axis=1)
        dq = dq_part_ref[i, qt].astype(jnp.float32) + dot(k_t, ds, NN)
        dq_ref[tile_rows(qt), HEADS[i]] = (dq * SCALE).T.astype(jnp.bfloat16)

    for qt in range(tiles):
        for i in range(GROUP):
            slopes(i, qt)
    for qt in range(tiles):
        for i in range(GROUP):
            back(i, qt)
    for j in range(tiles):
        units = [(i, qt) for qt in range(j, tiles) for i in range(GROUP)]
        at = [(i, qt * (qt + 1) // 2 + j) for i, qt in units]
        q_all = jnp.concatenate([q_ref[tile_rows(qt), HEADS[i]] for i, qt in units], axis=0)
        g_all = jnp.concatenate([g3_ref[i, qt] for i, qt in units], axis=1)
        p_all = jnp.concatenate([p_ref[a] for a in at], axis=1)
        ds_all = jnp.concatenate([ds_scr[a] for a in at], axis=1)
        sum_ref[tile_rows(j), HD:] += dot(p_all, g_all, NT)
        sum_ref[tile_rows(j), :HD] += dot(ds_all, q_all, NN) * SCALE


def call(kernel, grid, in_specs, out_specs, outs, scratch, flops, args, scalars=0, aliases={}):
    return pl.pallas_call(
        kernel,
        grid_spec=pltpu.PrefetchScalarGridSpec(
            num_scalar_prefetch=scalars,
            grid=grid,
            in_specs=in_specs,
            out_specs=out_specs,
            scratch_shapes=scratch,
        ),
        out_shape=outs,
        input_output_aliases=aliases,
        cost_estimate=pl.CostEstimate(flops=flops, bytes_accessed=16 * 2**20, transcendentals=0),
        compiler_params=pltpu.CompilerParams(vmem_limit_bytes=48 * 2**20),
    )(*args)


def shape(*dims, dtype=jnp.bfloat16):
    return jax.ShapeDtypeStruct(dims, dtype)


def forward_own(queries, sent, step0, steps, before=None):
    rows, width = queries.shape
    heads, tiles = width // HD, rows // TILE
    pairs = tiles * (tiles + 1) // 2
    work = steps * GROUP * pairs * TILE * TILE * HD
    by_unit = lambda a, r: pl.BlockSpec((GROUP, a, r, TILE), lambda h: (h + step0, 0, 0, 0))
    extra, after = ([], ()) if before is None else before
    return call(
        own_forward,
        (steps,),
        [pl.BlockSpec((rows, GROUP * HD), lambda h: (0, h + step0)), pl.BlockSpec(sent.shape, lambda h: (0, 0))]
        + [pl.BlockSpec(memory_space=pl.ANY)] * (len(extra) + len(after)),
        [by_unit(pairs, TILE), by_unit(tiles, HD), by_unit(tiles, 16)],
        [
            shape(heads, pairs, TILE, TILE),
            shape(heads, tiles, HD, TILE),
            shape(heads, tiles, 16, TILE, dtype=jnp.float32),
        ],
        [
            pltpu.VMEM((tiles, TILE, 2 * HD), jnp.bfloat16),
            pltpu.VMEM((tiles, HD + 16, TILE), jnp.bfloat16),
            pltpu.VMEM((tiles, TILE, HD), jnp.bfloat16),
            pltpu.VMEM((GROUP, tiles, tiles, TILE, TILE), jnp.float32),
        ],
        6 * work,
        (queries, sent, *extra, *after),
        aliases={2 + i: i for i in range(len(extra))},
    )


def earlier(queries, grad_out, first, part, stats, sent, chunks):
    rows, width = queries.shape
    heads, tiles, prev = width // HD, rows // TILE, len(chunks)
    max_n = prev * tiles * (TILE // KEYS)
    by_head = pl.BlockSpec((TILE, GROUP * HD), lambda h, t, s: (t, h))
    by_unit = lambda r: pl.BlockSpec((GROUP, 1, r, TILE), lambda h, t, s: (h, t, 0, 0))
    whole = lambda r: pl.BlockSpec((r, 2 * HD), lambda h, t, s: (0, 0))
    results = call(
        functools.partial(earlier_part, prev, max_n),
        (heads // GROUP, tiles),
        [by_head, by_head, by_unit(HD), by_unit(16)] + [whole(rows + 16)] * (prev + 1),
        [by_head, by_unit(HD), by_unit(8), by_unit(HD)] + [whole(rows)] * prev,
        [
            shape(rows, width),
            shape(heads, tiles, HD, TILE),
            shape(heads, tiles, 8, TILE, dtype=jnp.float32),
            shape(heads, tiles, HD, TILE),
        ]
        + [shape(rows, 2 * HD)] * prev,
        [
            pltpu.VMEM((max_n, KEYS, 2 * HD), jnp.bfloat16),
            pltpu.VMEM((max_n, HD, KEYS), jnp.bfloat16),
            pltpu.VMEM((max_n, KEYS, HD), jnp.bfloat16),
            pltpu.VMEM((max_n, HD + 16, KEYS), jnp.bfloat16),
            pltpu.VMEM((tiles, TILE, HD), jnp.bfloat16),
            pltpu.VMEM((GROUP, max_n, KEYS, TILE), jnp.float32),
            pltpu.VMEM((GROUP, max_n, KEYS, TILE), jnp.bfloat16),
            pltpu.VMEM((GROUP, max_n, KEYS, TILE), jnp.bfloat16),
            pltpu.VMEM((max_n, KEYS, HD), jnp.float32),
            pltpu.VMEM((max_n, KEYS, HD), jnp.float32),
            pltpu.SMEM((tiles,), jnp.int32),
        ],
        12 * heads * rows * max_n * KEYS * HD,
        (first, queries, grad_out, part, stats, sent, *chunks),
        scalars=1,
    )
    return results[:4], results[4:]


def backward_own(queries, sent, p_own, g3, delta, dq_part):
    rows, width = queries.shape
    heads, tiles = width // HD, rows // TILE
    pairs = tiles * (tiles + 1) // 2
    work = heads * pairs * TILE * TILE * HD
    by_head = pl.BlockSpec((rows, GROUP * HD), lambda h: (0, h))
    by_unit = lambda a, r: pl.BlockSpec((GROUP, a, r, TILE), lambda h: (h, 0, 0, 0))
    return call(
        own_backward,
        (heads // GROUP,),
        [
            by_head,
            pl.BlockSpec(sent.shape, lambda h: (0, 0)),
            by_unit(pairs, TILE),
            by_unit(tiles, HD),
            by_unit(tiles, 8),
            by_unit(tiles, HD),
        ],
        [by_head, pl.BlockSpec((rows, 2 * HD), lambda h: (0, 0))],
        [shape(rows, width), shape(rows, 2 * HD, dtype=jnp.float32)],
        [
            pltpu.VMEM((tiles, HD, TILE), jnp.bfloat16),
            pltpu.VMEM((GROUP, pairs, TILE, TILE), jnp.bfloat16),
        ],
        8 * work,
        (queries, sent, p_own, g3, delta, dq_part),
    )


def lay_out(copies, mixed_ref, dk_ref, dv_ref):
    for g in range(mixed_ref.shape[0] // copies):
        both = mixed_ref[g * copies].astype(jnp.float32)
        for c in range(1, copies):
            both = both + mixed_ref[g * copies + c].astype(jnp.float32)
        dk_ref[:, g * HD:(g + 1) * HD] = both[:, :HD].astype(jnp.bfloat16)
        dv_ref[:, g * HD:(g + 1) * HD] = both[:, HD:].astype(jnp.bfloat16)


def body(queries, keys, values, grad_out, doc_ids):
    tok_count = lax.axis_size("tok")
    head_count = lax.axis_size("head")
    rows = queries.shape[0]
    tiles = rows // TILE
    copy_count = head_count // KVH
    group = lax.axis_index("head") // copy_count
    longest = tok_count * rows // 2
    prev = min(tok_count - 1, -(-(longest - 1) // rows))
    docs = (doc_ids + 1).astype(jnp.bfloat16).reshape(tiles, TILE)
    sent = jnp.concatenate(
        [
            jnp.concatenate(
                [
                    lax.dynamic_slice_in_dim(keys, group * HD, HD, 1),
                    lax.dynamic_slice_in_dim(values, group * HD, HD, 1),
                ],
                axis=1,
            ),
            jnp.pad(docs, ((0, 16 - tiles), (0, 0))),
        ],
        axis=0,
    )
    first = (doc_ids + 1)[::TILE]
    shift_by = lambda x, k: lax.ppermute(
        x, "tok", [(i, i + k) for i in range(max(0, -k), min(tok_count, tok_count - k))]
    )
    steps = queries.shape[1] // (HD * GROUP)
    head_steps = (steps + 1) // 2
    own_part = forward_own(queries, sent, 0, head_steps)
    chunks = [shift_by(sent, 1)]
    own_part, chunks[0] = lax.optimization_barrier((own_part, chunks[0]))
    for _ in range(prev - 1):
        chunks.append(shift_by(chunks[-1], 1))
    if steps > head_steps:
        own_part = forward_own(queries, sent, head_steps, steps - head_steps, (own_part, chunks[:1]))
    p_own, part, stats = own_part
    chunks = chunks[::-1]
    (out, g3, delta, dq_part), sums = earlier(queries, grad_out, first, part, stats, sent, chunks)
    got = [shift_by(x, -k) for x, k in zip(sums, range(prev, 0, -1))]
    grad_q, total = backward_own(queries, sent, p_own, g3, delta, dq_part)
    for x in got:
        total = total + x.astype(jnp.float32)
    piece = rows // head_count
    mixed = lax.all_to_all(
        total.astype(jnp.bfloat16).reshape(head_count, piece, 2 * HD), "head", 0, 0, tiled=True
    )
    grad_k, grad_v = pl.pallas_call(
        functools.partial(lay_out, copy_count),
        out_shape=[shape(piece, KVH * HD)] * 2,
    )(mixed)
    return out, grad_q, grad_k, grad_v


def solution(mesh):
    return jax.shard_map(
        body,
        mesh=mesh,
        in_specs=(P("tok", "head"), P("tok", None), P("tok", None), P("tok", "head"), P("tok")),
        out_specs=(P("tok", "head"), P("tok", "head"), P(("tok", "head"), None), P(("tok", "head"), None)),
        check_vma=False,
    )
```
